256 devices in a mesh: dp: 4 (over y), expert: 64 (over z, x, core).
Axes of the slice: x: 4, y: 4, z: 8, core: 2. Of those that a mesh axis runs over, the one named last changes fastest.
Arguments:
- layer_inputs: bfloat16 [32768, 2048], P(('dp', 'expert')), may hold values from -6 to 6
- output_adjoint: bfloat16 [32768, 2048], P(('dp', 'expert')), may hold values from -6 to 6
- dispatcher_projection: bfloat16 [2048, 64], replicated, may hold values from -0.25 to 0.25
- gating_kernel: bfloat16 [2048, 128, 384], P('dp', 'expert'), may hold values from -0.125 to 0.125
- expansion_kernel: bfloat16 [2048, 128, 384], P('dp', 'expert'), may hold values from -0.125 to 0.125
- contraction_kernel: bfloat16 [2048, 128, 384], P('dp', 'expert'), may hold values from -0.3125 to 0.3125
- token_experts: int32 [32768, 8], P(('dp', 'expert')), may hold values from 0 to 63, all different within a row
- copy_choice_index: int32 [32768, 8], P(('dp', 'expert')), may hold values from 0 to 3
- expert_copies: int32 [64, 4], replicated, may hold values from 0 to 127, as said below
- send_quotas: int32 [128], replicated, may hold values from 3 to 5, as said below
Outputs:
- token_grad: bfloat16 [32768, 2048], P(('dp', 'expert'))
- gate_grad: float32 [2048, 128, 384], P('dp', 'expert')
- up_grad: float32 [2048, 128, 384], P('dp', 'expert')
- down_grad: float32 [2048, 128, 384], P('dp', 'expert')
- router_grad: float32 [2048, 64], P('dp', 'expert')
The draws below stay inside these ranges and needn't reach their ends.
Inputs may be any that keep to these rules, and one draw needn't show every extreme that they name: `expert_copies`: row e lists slots that hold expert e, repeats allowed, starting with slot e * 2; every slot appears in exactly one row. `send_quotas`: some slot has capacity exactly 5.
All inputs are finite; a program needn't handle non-finite values.
Results may differ from the reference program's by a relative error of at most 0.017.
Values may be sent and summed in bfloat16 or wider, within the bound.
A program may use at most 128 MiB of HBM per device.

```python
import jax
import jax.numpy as jnp
from jax import lax

D = 2048
FF = 384
TOP = 8
SLOT_DEV = 2
REPL = 4
CAP = 5
TOK_DEV = 128
EXPERTS = 64
SLOTS = 128
TOKENS = 32768
N_DP = 4
N_EXPERT = 64


def draw_expert_copies(key, part):
    key = jax.random.fold_in(key, 11)
    shuffled = jax.random.permutation(key, EXPERTS)
    standing = jnp.argsort(shuffled, stable=True).astype(jnp.int32)
    expert_ids = jnp.arange(EXPERTS, dtype=jnp.int32)
    primary = expert_ids * SLOT_DEV
    chosen_hot = standing < EXPERTS // 2
    first_spare = jnp.where(chosen_hot, 2 * standing * SLOT_DEV + 1, primary)
    second_spare = jnp.where(chosen_hot, (2 * standing + 1) * SLOT_DEV + 1, primary)
    return jnp.stack([primary, first_spare, second_spare, primary], axis=1).astype(jnp.int32)


def draw_send_quotas(key, part):
    key = jax.random.fold_in(key, 23)
    first_key, second_key = jax.random.split(key)
    limits = jax.random.randint(first_key, (SLOTS,), CAP * 2 // 3, CAP + 1)
    target = jax.random.randint(second_key, (), 0, SLOTS)
    return limits.at[target].set(CAP).astype(jnp.int32)


def set_ends(entries, key, smallest, high):
    dims = entries.shape
    index_at = [jax.random.randint(jax.random.fold_in(key, axis), (), 0, dims[axis]) for axis in range(len(dims))]
    entries = entries.at[tuple(index_at)].set(smallest)
    longest = dims.index(max(dims))
    index_at[longest] = (index_at[longest] + 1) % dims[longest]
    return entries.at[tuple(index_at)].set(high)


def levels(key, extent, cuts, least, largest):
    def one(dim, shards_of):
        steps = jax.random.uniform(jax.random.fold_in(jax.random.fold_in(key, 6), dim), (shards_of,), jnp.float32, least / len(cuts), largest / len(cuts))
        return jnp.repeat(jnp.exp(steps), extent[dim] // shards_of).reshape((-1,) + (1,) * (len(extent) - dim - 1))

    level = one(*cuts[0])
    for cut in cuts[1:]:
        level = level * one(*cut)
    return level


def choose_distinct(own_key, rows, count, top, lift):
    sequence = jax.random.permutation(jax.random.fold_in(own_key, 1), count)
    boost = sequence
    for power in range(3):
        boost = boost * boost // count
    boost = boost * lift // count
    lots = jax.random.randint(jax.random.fold_in(own_key, 2), (rows, count), 0, 4096) + boost
    sure = jax.random.permutation(jax.random.fold_in(own_key, 3), rows)[jnp.arange(count) % rows]
    lots = jnp.where(jnp.arange(rows)[:, None] == sure[None, :], 1 << 14, lots)
    score = lots * count + jnp.arange(count)
    return lax.top_k(score.astype(jnp.int32), top)[1].astype(jnp.int32)


def scatter_about(key, shape, deviation, reach, shards=(), kind=jnp.bfloat16):
    entries = jax.random.normal(key, shape, jnp.float32) * deviation
    if len(shards) > 0:
        entries = levels(key, shape, shards, -0.22, 0.18) * entries
    return jnp.clip(entries, min=-reach, max=reach).astype(kind)


def setup_inputs(seed: int = 0) -> dict:
    arg_keys = jax.random.split(jax.random.key(seed), 11)
    layer_inputs = scatter_about(arg_keys[0], (TOKENS, D), 1.0, 6.0, ((0, 256),))
    output_adjoint = scatter_about(arg_keys[1], (TOKENS, D), 1.0, 6.0, ((0, 256),))
    dispatcher_projection = scatter_about(arg_keys[2], (D, EXPERTS), (D // 4) ** -0.5, 0.25)
    gating_kernel = scatter_about(arg_keys[3], (D, SLOTS, FF), D ** -0.5, 0.125, ((0, 4), (1, 64)))
    expansion_kernel = scatter_about(arg_keys[4], (D, SLOTS, FF), D ** -0.5, 0.125, ((0, 4), (1, 64)))
    contraction_kernel = scatter_about(arg_keys[5], (D, SLOTS, FF), FF ** -0.5, 0.3125, ((0, 4), (1, 64)))
    token_experts = choose_distinct(arg_keys[6], TOKENS, EXPERTS, TOP, 2048)
    copy_choice_index = set_ends(jax.random.randint(arg_keys[7], (TOKENS, TOP), 0, REPL), jax.random.fold_in(arg_keys[7], 1), 0, REPL - 1).astype(jnp.int32)
    expert_copies = draw_expert_copies(jax.random.fold_in(arg_keys[10], 71), 0)
    send_quotas = draw_send_quotas(jax.random.fold_in(arg_keys[10], 71), 0)
    return dict(layer_inputs=layer_inputs, output_adjoint=output_adjoint, dispatcher_projection=dispatcher_projection, gating_kernel=gating_kernel, expansion_kernel=expansion_kernel, contraction_kernel=contraction_kernel, token_experts=token_experts, copy_choice_index=copy_choice_index, expert_copies=expert_copies, send_quotas=send_quotas)


def tile_arrangement(tile_assignments, tile_picks, expert_copies, send_quotas):
    fanout = tile_assignments.shape[1]
    pair_count = tile_assignments.shape[0] * fanout
    experts = expert_copies.shape[0]
    replicas = expert_copies.shape[1]
    position_count = send_quotas.shape[0]
    flat_pick = (tile_assignments * replicas + tile_picks).reshape(pair_count)
    replica_table = expert_copies.reshape(experts * replicas)
    target = jnp.sum(jnp.where(flat_pick[:, None] == jnp.arange(experts * replicas, dtype=jnp.int32)[None, :], replica_table[None, :], 0), axis=1).astype(jnp.int32)
    position_agrees = (target[:, None] == jnp.arange(position_count, dtype=jnp.int32)[None, :]).astype(jnp.int32)
    arrival = jnp.sum((jnp.cumsum(position_agrees, axis=0) - position_agrees) * position_agrees, axis=1).astype(jnp.int32)
    position_bound = jnp.sum(position_agrees * send_quotas[None, :], axis=1).astype(jnp.int32)
    position = jnp.where(arrival < position_bound, target * CAP + arrival, position_count * CAP).astype(jnp.int32)
    source_pair = jnp.full((position_count * CAP,), pair_count, jnp.int32)
    return source_pair.at[position].set(jnp.arange(pair_count, dtype=jnp.int32), mode="drop")


def reference(layer_inputs, output_adjoint, dispatcher_projection, gating_kernel, expansion_kernel, contraction_kernel, token_experts, copy_choice_index, expert_copies, send_quotas):
    blocks = N_DP * N_EXPERT
    block_pairs = TOK_DEV * TOP
    logits = jnp.dot(layer_inputs, dispatcher_projection, preferred_element_type=jnp.float32)
    route_hit = token_experts[:, :, None] == jnp.arange(EXPERTS, dtype=jnp.int32)[None, None, :]
    chosen = jnp.sum(jnp.where(route_hit, logits[:, None, :], jnp.float32(0.0)), axis=2)
    probs = jax.nn.softmax(chosen, axis=1)
    sent_prob = probs.astype(jnp.bfloat16)
    arrangement_sequence = lax.map(lambda present_item: tile_arrangement(present_item[0], present_item[1], expert_copies, send_quotas),
                    (token_experts.reshape(blocks, TOK_DEV, TOP), copy_choice_index.reshape(blocks, TOK_DEV, TOP)))
    offset = (jnp.arange(blocks, dtype=jnp.int32) * block_pairs)[:, None]
    global_pair = jnp.where(arrangement_sequence < block_pairs, arrangement_sequence + offset, TOKENS * TOP).astype(jnp.int32)
    order = global_pair.reshape(N_DP, N_EXPERT, SLOTS, CAP).transpose(2, 0, 1, 3).reshape(SLOTS, N_DP, N_EXPERT * CAP)
    token_pad = jnp.concatenate([layer_inputs, jnp.zeros((1, D), jnp.bfloat16)], axis=0)
    cot_pad = jnp.concatenate([output_adjoint, jnp.zeros((1, D), jnp.bfloat16)], axis=0)
    prob_pad = jnp.concatenate([sent_prob.reshape(TOKENS * TOP), jnp.zeros((1,), jnp.bfloat16)])

    def per_slot(partial_value, present_item):
        dx_acc, grad_acc = partial_value
        ids, wg, wu, wd = present_item
        summed = jnp.zeros((D, 3 * FF), jnp.float32)
        for index in range(N_DP):
            pair_ids = ids[index]
            token_ids = (pair_ids // TOP).astype(jnp.int32)
            slot_rows = token_pad[token_ids]
            slot_cot = cot_pad[token_ids]
            slot_prob = prob_pad[pair_ids].astype(jnp.float32)
            gate_value = jnp.dot(slot_rows, wg, preferred_element_type=jnp.float32)
            up_value = jnp.dot(slot_rows, wu, preferred_element_type=jnp.float32)
            down_back = jnp.dot(slot_cot, wd, preferred_element_type=jnp.float32)
            sigmoid_gate = jax.nn.sigmoid(gate_value)
            silu_gate = gate_value * sigmoid_gate
            activation = (silu_gate * up_value).astype(jnp.bfloat16)
            pair_grad = jnp.sum(activation.astype(jnp.float32) * down_back, axis=1).astype(jnp.bfloat16)
            out_grad = (slot_prob[:, None] * slot_cot.astype(jnp.float32)).astype(jnp.bfloat16)
            act_grad = slot_prob[:, None] * down_back
            gate_part = (act_grad * up_value * sigmoid_gate * (1.0 + gate_value * (1.0 - sigmoid_gate))).astype(jnp.bfloat16)
            up_part = (act_grad * silu_gate).astype(jnp.bfloat16)
            pair_dx = (jnp.dot(gate_part, wg.T, preferred_element_type=jnp.float32)
                       + jnp.dot(up_part, wu.T, preferred_element_type=jnp.float32)).astype(jnp.bfloat16)
            piece = jnp.concatenate([jnp.dot(slot_rows.T, gate_part, preferred_element_type=jnp.float32),
                                     jnp.dot(slot_rows.T, up_part, preferred_element_type=jnp.float32),
                                     jnp.dot(out_grad.T, activation, preferred_element_type=jnp.float32)], axis=1)
            summed = summed + piece.astype(jnp.bfloat16).astype(jnp.float32)
            dx_acc = dx_acc.at[token_ids].add(pair_dx.astype(jnp.float32))
            grad_acc = grad_acc.at[pair_ids].add(pair_grad.astype(jnp.float32))
        return (dx_acc, grad_acc), summed

    start = (jnp.zeros((TOKENS + 1, D), jnp.float32), jnp.zeros((TOKENS * TOP + 1,), jnp.float32))
    (dx_acc, grad_acc), stacked = lax.scan(per_slot, start, (order, gating_kernel.transpose(1, 0, 2), expansion_kernel.transpose(1, 0, 2), contraction_kernel.transpose(1, 0, 2)))
    gate_grad = stacked[:, :, :FF].transpose(1, 0, 2)
    up_grad = stacked[:, :, FF:2 * FF].transpose(1, 0, 2)
    down_grad = stacked[:, :, 2 * FF:].transpose(1, 0, 2)
    pair_dp = grad_acc[:TOKENS * TOP].reshape(TOKENS, TOP)
    weighted = jnp.sum(probs * pair_dp, axis=1, keepdims=True)
    chosen_grad = probs * (pair_dp - weighted)
    logit_grad = jnp.sum(jnp.where(route_hit, chosen_grad[:, :, None], jnp.float32(0.0)), axis=1).astype(jnp.bfloat16)
    token_grad = (dx_acc[:TOKENS] + jnp.dot(logit_grad, dispatcher_projection.T, preferred_element_type=jnp.float32)).astype(jnp.bfloat16)
    router_grad = jnp.dot(layer_inputs.T, logit_grad, preferred_element_type=jnp.float32)
    return token_grad, gate_grad, up_grad, down_grad, router_grad
```

```python
import jax
import jax.numpy as jnp
from jax import lax
from jax.sharding import PartitionSpec as P

CAP = 5


def contract(operand, weights):
    return jnp.einsum("srd,dsf->srf", operand, weights, preferred_element_type=jnp.float32)


def expand(gradients, weights):
    return jnp.einsum("srf,dsf->srd", gradients, weights, preferred_element_type=jnp.float32)


def outer_sum(operand, gradients):
    return jnp.einsum("srd,srf->dsf", operand, gradients, preferred_element_type=jnp.float32)


def shards(
    layer_inputs,
    output_adjoint,
    dispatcher_projection,
    gating_kernel,
    expansion_kernel,
    contraction_kernel,
    token_experts,
    copy_choice_index,
    expert_copies,
    send_quotas,
):
    tok_rows = layer_inputs.shape[0]
    model_width = layer_inputs.shape[1]
    fanout = token_experts.shape[1]
    experts = dispatcher_projection.shape[1]
    replicas = expert_copies.shape[1]
    position_count = send_quotas.shape[0]
    local_slots = gating_kernel.shape[1]
    hidden = gating_kernel.shape[2]
    expert_devs = lax.axis_size("expert")
    pair_count = tok_rows * fanout
    slot_len = expert_devs * CAP
    buffer_len = local_slots * slot_len
    logits = jnp.dot(layer_inputs, dispatcher_projection, preferred_element_type=jnp.float32)
    route_hit = token_experts[:, :, None] == lax.iota(jnp.int32, experts)[None, None, :]
    chosen = jnp.sum(jnp.where(route_hit, logits[:, None, :], 0.0), axis=2)
    probs = jax.nn.softmax(chosen, axis=1)
    flat_pick = (token_experts * replicas + copy_choice_index).reshape(pair_count)
    replica_table = expert_copies.reshape(experts * replicas)
    target = jnp.sum(
        jnp.where(
            flat_pick[:, None] == lax.iota(jnp.int32, experts * replicas)[None, :],
            replica_table[None, :],
            0,
        ),
        axis=1,
    )
    position_agrees = (target[:, None] == lax.iota(jnp.int32, position_count)[None, :]).astype(
        jnp.int32
    )
    arrival = jnp.sum(
        (jnp.cumsum(position_agrees, axis=0) - position_agrees) * position_agrees, axis=1
    )
    position_bound = jnp.sum(position_agrees * send_quotas[None, :], axis=1)
    owner_dev = target // local_slots
    place_slot = target % local_slots
    position = jnp.where(
        arrival < position_bound, (place_slot * expert_devs + owner_dev) * CAP + arrival, buffer_len
    )
    pick = position[None, :] == lax.iota(jnp.int32, buffer_len)[:, None]
    send_prob = jnp.sum(
        jnp.where(pick, probs.astype(jnp.bfloat16).astype(jnp.float32).reshape(1, pair_count), 0.0),
        axis=1,
    ).astype(jnp.bfloat16)
    chosen_row = jnp.any(pick.reshape(buffer_len, tok_rows, fanout), axis=2).astype(jnp.bfloat16)
    send_rows = jnp.dot(chosen_row, layer_inputs, preferred_element_type=jnp.bfloat16)
    send_cot = jnp.dot(chosen_row, output_adjoint, preferred_element_type=jnp.bfloat16)
    send_rows = send_rows.reshape(local_slots, expert_devs, CAP, model_width)
    send_cot = send_cot.reshape(local_slots, expert_devs, CAP, model_width)
    send_prob = send_prob.reshape(local_slots, expert_devs, CAP)
    got_rows, got_cot, got_prob = (
        lax.all_to_all(send_rows, "expert", split_axis=1, concat_axis=1, tiled=True),
        lax.all_to_all(send_cot, "expert", split_axis=1, concat_axis=1, tiled=True),
        lax.all_to_all(send_prob, "expert", split_axis=1, concat_axis=1, tiled=True),
    )
    slot_rows = got_rows.reshape(local_slots, slot_len, model_width)
    slot_cot = got_cot.reshape(local_slots, slot_len, model_width)
    slot_prob = got_prob.reshape(local_slots, slot_len).astype(jnp.float32)
    pieces = (
        lax.all_gather(gating_kernel, "dp", axis=0, tiled=True),
        lax.all_gather(expansion_kernel, "dp", axis=0, tiled=True),
        lax.all_gather(contraction_kernel, "dp", axis=0, tiled=True),
    )
    row_part = slot_rows
    gate_value = contract(row_part, pieces[0])
    up_value = contract(row_part, pieces[1])
    down_back = contract(slot_cot, pieces[2])
    sigmoid_gate = jax.nn.sigmoid(gate_value)
    silu_gate = gate_value * sigmoid_gate
    activation = (silu_gate * up_value).astype(jnp.bfloat16)
    pair_grad = jnp.sum(activation.astype(jnp.float32) * down_back, axis=2).astype(jnp.bfloat16)
    out_grad = (slot_prob[:, :, None] * slot_cot.astype(jnp.float32)).astype(jnp.bfloat16)
    act_grad = slot_prob[:, :, None] * down_back
    gate_part = (
        act_grad * up_value * sigmoid_gate * (1.0 + gate_value * (1.0 - sigmoid_gate))
    ).astype(jnp.bfloat16)
    up_part = (act_grad * silu_gate).astype(jnp.bfloat16)
    pair_dx = (expand(gate_part, pieces[0]) + expand(up_part, pieces[1])).astype(jnp.bfloat16)
    row_part = slot_rows
    summed = lax.psum_scatter(
        jnp.concatenate(
            [
                outer_sum(row_part, gate_part),
                outer_sum(row_part, up_part),
                outer_sum(out_grad, activation),
            ],
            axis=2,
        ).astype(jnp.bfloat16),
        "dp",
        scatter_dimension=0,
        tiled=True,
    ).astype(jnp.float32)
    gate_grad = summed[:, :, :hidden]
    up_grad = summed[:, :, hidden : 2 * hidden]
    down_grad = summed[:, :, 2 * hidden :]
    back_rows, back_grad = (
        lax.all_to_all(
            pair_dx.reshape(local_slots, expert_devs, CAP, model_width),
            "expert",
            split_axis=1,
            concat_axis=1,
            tiled=True,
        ),
        lax.all_to_all(
            pair_grad.reshape(local_slots, expert_devs, CAP),
            "expert",
            split_axis=1,
            concat_axis=1,
            tiled=True,
        ),
    )
    dx_sum = jnp.dot(
        chosen_row.T,
        back_rows.reshape(buffer_len, model_width),
        preferred_element_type=jnp.float32,
    )
    pair_dp = jnp.sum(
        jnp.where(pick, back_grad.astype(jnp.float32).reshape(buffer_len, 1), 0.0), axis=0
    ).reshape(tok_rows, fanout)
    weighted = jnp.sum(probs * pair_dp, axis=1, keepdims=True)
    chosen_grad = probs * (pair_dp - weighted)
    logit_grad = jnp.sum(jnp.where(route_hit, chosen_grad[:, :, None], 0.0), axis=1).astype(
        jnp.bfloat16
    )
    token_grad = (
        dx_sum + jnp.dot(logit_grad, dispatcher_projection.T, preferred_element_type=jnp.float32)
    ).astype(jnp.bfloat16)
    router_term = jnp.dot(layer_inputs.T, logit_grad, preferred_element_type=jnp.float32)
    columns = lax.all_to_all(router_term.T, "expert", split_axis=0, concat_axis=0, tiled=True)
    router_grad = lax.psum_scatter(
        jnp.sum(columns, axis=0), "dp", scatter_dimension=0, tiled=True
    )[:, None]
    return (token_grad, gate_grad, up_grad, down_grad, router_grad)


def solution(mesh):
    return jax.shard_map(
        shards,
        mesh=mesh,
        in_specs=(
            P(("dp", "expert"), None),
            P(("dp", "expert"), None),
            P(),
            P("dp", "expert", None),
            P("dp", "expert", None),
            P("dp", "expert", None),
            P(("dp", "expert"), None),
            P(("dp", "expert"), None),
            P(),
            P(),
        ),
        out_specs=(
            P(("dp", "expert"), None),
            P("dp", "expert", None),
            P("dp", "expert", None),
            P("dp", "expert", None),
            P("dp", "expert"),
        ),
        check_vma=False,
    )
```

```python
import functools

import jax
import jax.numpy as jnp
from jax import lax
from jax.experimental import pallas as pl
from jax.experimental.pallas import tpu as pltpu
from jax.sharding import PartitionSpec as P

CAP = 5
LANES = 128
MESH = pl.DeviceIdType.MESH
F32 = jnp.float32
BF16 = jnp.bfloat16


def dispatch_kernel(pick, x_ref, g_ref, out_ref, flat):
    tokens, width = x_ref.shape
    slabs = width // LANES
    slots, devs, depth = out_ref.shape[:3]
    cap = depth // 2
    flat[pl.ds(tokens * slabs, slabs), :] = jnp.zeros((slabs, LANES), F32)
    for which, ref in enumerate((x_ref, g_ref)):
        for a in range(slabs):
            flat[pl.ds(a, tokens, stride=slabs), :] = ref[:, a * LANES : (a + 1) * LANES].astype(F32)

        def one(d, carry, which=which):
            for s in range(slots):
                for c in range(cap):
                    token = pick[(s * devs + d) * cap + c]
                    row = pl.multiple_of(token * slabs, slabs)
                    out_ref[s, d, which * cap + c] = flat[pl.ds(row, slabs), :].astype(BF16)
            return carry

        lax.fori_loop(0, devs, one, 0)


def combine_kernel(place, back_ref, lg_ref, proj_ref, out_ref, flat):
    tokens, width = out_ref.shape
    slabs = width // LANES
    fanout = place.shape[0] // tokens

    def one(t, carry):
        total = back_ref[place[t * fanout]].astype(F32)
        for k in range(1, fanout):
            total = total + back_ref[place[t * fanout + k]].astype(F32)
        flat[pl.ds(pl.multiple_of(t * slabs, slabs), slabs), :] = total
        return carry

    lax.fori_loop(0, tokens, one, 0)
    for a in range(slabs):
        cols = slice(a * LANES, (a + 1) * LANES)
        routed = lax.dot_general(
            lg_ref[...], proj_ref[cols, :], (((1,), (1,)), ((), ())), preferred_element_type=F32
        )
        out_ref[:, cols] = (flat[pl.ds(a, tokens, stride=slabs), :] + routed).astype(BF16)


def exchange_kernel(
    n_dp,
    n_exp,
    send,
    q_send,
    w,
    x,
    te,
    dev,
    lane,
    probs,
    back,
    dw,
    lg_out,
    rcol,
    recv,
    q_recv,
    wf,
    flat,
    xm,
    gm,
    gu,
    act_s,
    dwp,
    rs1,
    rs2,
    dxs,
    zero,
    pg,
    pg_recv,
    rt,
    rt_recv,
    r2,
    tok_ss,
    tok_rs,
    q_ss,
    q_rs,
    w_ss,
    w_rs,
    g_ss,
    g_rs,
    dx_ss,
    dx_rs,
    pg_ss,
    pg_rs,
    rt_ss,
    rt_rs,
    r2_ss,
    r2_rs,
    own_sem,
):
    me = lax.axis_index("expert")
    my = lax.axis_index("dp")
    right = lax.rem(my + 1, n_dp)
    far = lax.rem(my + 2, n_dp)
    left = lax.rem(my + 3, n_dp)
    slots, _, depth, slabs, _ = recv.shape
    cap = depth // 2
    rows = cap * n_exp
    quarter = wf.shape[2]
    half = quarter // 2
    ff = wf.shape[3] // 3
    per = slabs // n_dp
    chunk = min(8, n_exp)
    others = n_exp - 1

    barrier = pltpu.get_barrier_semaphore()

    def greet(i, carry):
        pl.semaphore_signal(
            barrier, inc=1, device_id={"expert": lax.rem(me + i, n_exp)}, device_id_type=MESH
        )
        return carry

    lax.fori_loop(1, n_exp, greet, 0)
    for other in (right, far, left):
        pl.semaphore_signal(barrier, inc=1, device_id={"dp": other}, device_id_type=MESH)
    pl.semaphore_wait(barrier, others + n_dp - 1)

    def to_dp(src, dst, ss, rs, other):
        return pltpu.make_async_remote_copy(
            src, dst, ss, rs, device_id={"dp": other}, device_id_type=MESH
        )

    def to_exp(src, dst, ss, rs, other):
        return pltpu.make_async_remote_copy(
            src, dst, ss, rs, device_id={"expert": other}, device_id_type=MESH
        )

    def to_all(make):
        def one(i, carry):
            make(lax.rem(me + i, n_exp)).start()
            return carry

        lax.fori_loop(1, n_exp, one, 0)

    def wait_for(ref, sem):
        pltpu.make_async_copy(ref, ref, sem).wait()

    def w_first(s):
        for n, other in enumerate((right, left)):
            to_dp(w.at[s], wf.at[s, my], w_ss.at[s, n], w_rs.at[s, n], other).start()

    def w_second(s):
        wait_for(wf.at[s, left], w_rs.at[s, 0])
        part = wf.at[s, left, pl.ds(0, half)]
        to_dp(part, part, w_ss.at[s, 2], w_rs.at[s, 2], right).start()
        wait_for(wf.at[s, right], w_rs.at[s, 1])
        part = wf.at[s, right, pl.ds(half, half)]
        to_dp(part, part, w_ss.at[s, 3], w_rs.at[s, 3], left).start()

    def w_end(s):
        wait_for(wf.at[s, far, pl.ds(0, half)], w_rs.at[s, 2])
        wait_for(wf.at[s, far, pl.ds(half, half)], w_rs.at[s, 3])

    w_first(0)
    own = [pltpu.make_async_copy(w.at[s], wf.at[s, my], own_sem.at[s]) for s in range(slots)]
    own += [
        pltpu.make_async_copy(send.at[s, me], recv.at[s, me], own_sem.at[slots + s])
        for s in range(slots)
    ]
    for copy in own:
        copy.start()
    to_all(lambda d: to_exp(send.at[0, d], recv.at[0, me], tok_ss.at[0], tok_rs.at[0], d))
    to_all(lambda d: to_exp(q_send.at[d], q_recv.at[me], q_ss, q_rs, d))
    to_all(lambda d: to_exp(send.at[1, d], recv.at[1, me], tok_ss.at[1], tok_rs.at[1], d))
    q_recv[me] = q_send[me]
    zero[...] = jnp.zeros_like(zero)
    zero_copy = pltpu.make_async_copy(zero, back.at[slots * rows], own_sem.at[2 * slots])
    zero_copy.start()
    w_second(0)
    w_first(1)

    def to_matrix(s, which, out):
        def unpack(i, carry):
            block = recv[s, pl.ds(i * chunk, chunk), which * cap : (which + 1) * cap]
            size = chunk * cap * slabs
            flat[pl.ds(pl.multiple_of(i * size, size), size), :] = block.astype(F32).reshape(
                size, LANES
            )
            return carry

        lax.fori_loop(0, n_exp // chunk, unpack, 0)

        def gather(p, carry):
            for b in range(per):
                for c in range(cap):
                    part = flat[pl.ds(c * slabs + p * per + b, n_exp, stride=cap * slabs), :]
                    out[p, c * n_exp : (c + 1) * n_exp, b * LANES : (b + 1) * LANES] = part.astype(
                        BF16
                    )
            return carry

        lax.fori_loop(0, n_dp, gather, 0)

    lanes = lax.broadcasted_iota(jnp.int32, (n_exp, LANES), 1)

    def weight_of(s):
        table = q_recv[...].reshape(n_exp, LANES)
        return jnp.concatenate(
            [table[:, s * cap + c : s * cap + c + 1] for c in range(cap)], axis=0
        )

    def forward(s):
        to_matrix(s, 0, xm)
        to_matrix(s, 1, gm)

        def project(p, carry):
            gate_up, down = carry
            gate_up = gate_up + jnp.dot(
                xm[p], wf[s, p, :, : 2 * ff], preferred_element_type=F32
            )
            down = down + jnp.dot(gm[p], wf[s, p, :, 2 * ff :], preferred_element_type=F32)
            return gate_up, down

        gate_up, down = lax.fori_loop(
            0, n_dp, project, (jnp.zeros((rows, 2 * ff), F32), jnp.zeros((rows, ff), F32))
        )
        gate, up = gate_up[:, :ff], gate_up[:, ff:]
        sig = jax.nn.sigmoid(gate)
        silu = gate * sig
        act = (silu * up).astype(BF16)
        act_s[...] = act
        grad = jnp.sum(act.astype(F32) * down, axis=1, keepdims=True).astype(BF16).astype(F32)
        act_grad = weight_of(s) * down
        gu[:, :ff] = (act_grad * up * sig * (1.0 + gate * (1.0 - sig))).astype(BF16)
        gu[:, ff:] = (act_grad * silu).astype(BF16)
        table = jnp.zeros((n_exp, LANES), F32)
        for c in range(cap):
            table = jnp.where(
                lanes == s * cap + c, grad[c * n_exp : (c + 1) * n_exp], table
            )
        return table

    def weight_grad(s, p):
        both = (((0,), (0,)), ((), ()))
        dwp[s, p, :, : 2 * ff] = lax.dot_general(
            xm[p], gu[...], both, preferred_element_type=F32
        ).astype(BF16)
        out_grad = (weight_of(s) * gm[p].astype(F32)).astype(BF16)
        dwp[s, p, :, 2 * ff :] = lax.dot_general(
            out_grad, act_s[...], both, preferred_element_type=F32
        ).astype(BF16)

    def input_grad(s):
        def one(p, carry):
            value = lax.dot_general(
                gu[...],
                wf[s, p, :, : 2 * ff],
                (((1,), (1,)), ((), ())),
                preferred_element_type=F32,
            )
            for b in range(per):
                for c in range(cap):
                    flat[pl.ds(c * slabs + p * per + b, n_exp, stride=cap * slabs), :] = value[
                        c * n_exp : (c + 1) * n_exp, b * LANES : (b + 1) * LANES
                    ]
            return carry

        lax.fori_loop(0, n_dp, one, 0)

        def pack(i, carry):
            size = chunk * cap * slabs
            block = flat[pl.ds(pl.multiple_of(i * size, size), size), :]
            dxs[s, pl.ds(i * chunk, chunk)] = block.astype(BF16).reshape(chunk, cap, slabs, LANES)
            return carry

        lax.fori_loop(0, n_exp // chunk, pack, 0)

    def place(s, d):
        return back.at[pl.ds((s * n_exp + d) * cap, cap)]

    def dx_start(s):
        pltpu.make_async_copy(dxs.at[s, me], place(s, me), own_sem.at[2 * slots + 1 + s]).start()
        to_all(lambda d: to_exp(dxs.at[s, d], place(s, me), dx_ss.at[s], dx_rs.at[s], d))

    def sum_first(s):
        to_dp(
            dwp.at[s, far, pl.ds(0, half)], rs1.at[s, 0], g_ss.at[s, 0], g_rs.at[s, 0], right
        ).start()
        to_dp(
            dwp.at[s, far, pl.ds(half, half)], rs1.at[s, 1], g_ss.at[s, 1], g_rs.at[s, 1], left
        ).start()

    def sum_second(s):
        for n, other in enumerate((right, left)):
            wait_for(rs1.at[s, n], g_rs.at[s, n])
            part = pl.ds(n * half, half)
            dwp[s, other, part] = (
                dwp[s, other, part].astype(F32) + rs1[s, n].astype(F32)
            ).astype(BF16)
            to_dp(
                dwp.at[s, other], rs2.at[s, n], g_ss.at[s, 2 + n], g_rs.at[s, 2 + n], other
            ).start()

    def sum_end(s):
        wait_for(rs2.at[s, 0], g_rs.at[s, 2])
        wait_for(rs2.at[s, 1], g_rs.at[s, 3])
        dw[s] = dwp[s, my].astype(F32) + rs2[s, 0].astype(F32) + rs2[s, 1].astype(F32)

    def tokens_here(s):
        wait_for(recv.at[s, pl.ds(0, others)], tok_rs.at[s])
        own[slots + s].wait()

    tokens_here(0)
    wait_for(q_recv.at[pl.ds(0, others)], q_rs)
    own[0].wait()
    w_end(0)
    table = forward(0)
    weight_grad(0, far)
    sum_first(0)
    w_second(1)
    weight_grad(0, right)
    weight_grad(0, left)
    weight_grad(0, my)
    input_grad(0)
    sum_second(0)
    own[1].wait()
    w_end(1)

    tokens_here(1)
    dx_start(0)
    table = table + forward(1)
    pg[...] = table.reshape(pg.shape)
    to_all(lambda d: to_exp(pg.at[d], pg_recv.at[me], pg_ss, pg_rs, d))
    pg_recv[me] = pg[me]
    weight_grad(1, far)
    sum_first(1)
    weight_grad(1, right)
    weight_grad(1, left)
    weight_grad(1, my)
    input_grad(1)
    dx_start(1)
    sum_second(1)

    wait_for(pg_recv.at[pl.ds(0, others)], pg_rs)
    grads = pg_recv[...].reshape(n_exp, LANES).astype(BF16)
    tokens, fanout = te.shape
    dev_ids = lax.broadcasted_iota(jnp.int32, (tokens, n_exp), 1)
    lane_ids = lax.broadcasted_iota(jnp.int32, (tokens, LANES), 1)
    pair = []
    weighted = jnp.zeros((tokens, 1), F32)
    for k in range(fanout):
        hit = (dev[:, k : k + 1] == dev_ids).astype(F32).astype(BF16)
        spread = jnp.dot(hit, grads, preferred_element_type=F32)
        value = jnp.sum(
            jnp.where(lane[:, k : k + 1] == lane_ids, spread, 0.0), axis=1, keepdims=True
        )
        pair.append(value)
        weighted = weighted + probs[:, k : k + 1] * value
    logit = jnp.zeros((tokens, n_exp), F32)
    for k in range(fanout):
        chosen = probs[:, k : k + 1] * (pair[k] - weighted)
        logit = logit + jnp.where(te[:, k : k + 1] == dev_ids, chosen, 0.0)
    logit = logit.astype(BF16)
    lg_out[...] = logit
    for a in range(slabs):
        flat[pl.ds(a, n_exp, stride=slabs), :] = lax.dot_general(
            logit,
            x[:, a * LANES : (a + 1) * LANES],
            (((0,), (0,)), ((), ())),
            preferred_element_type=F32,
        )
    rt[...] = flat[pl.ds(0, n_exp * slabs), :].astype(BF16).reshape(rt.shape)
    to_all(lambda d: to_exp(rt.at[d], rt_recv.at[me], rt_ss, rt_rs, d))
    rt_recv[me] = rt[me]
    sum_end(0)
    wait_for(rt_recv.at[pl.ds(0, others)], rt_rs)
    r2[0] = jnp.sum(rt_recv[...].astype(F32), axis=0)
    for n, other in enumerate((right, far, left)):
        to_dp(r2.at[0], r2.at[n + 1], r2_ss.at[n], r2_rs.at[n], other).start()
    for n in range(n_dp - 1):
        wait_for(r2.at[n + 1], r2_rs.at[n])
    rcol[...] = r2[0] + r2[1] + r2[2] + r2[3]
    sum_end(1)

    zero_copy.wait()
    wait_for(q_send.at[pl.ds(0, others)], q_ss)
    wait_for(pg.at[pl.ds(0, others)], pg_ss)
    wait_for(rt.at[pl.ds(0, others)], rt_ss)
    for n in range(n_dp - 1):
        wait_for(r2.at[0], r2_ss.at[n])
    for s in range(slots):
        wait_for(recv.at[s, pl.ds(0, others)], tok_ss.at[s])
        wait_for(wf.at[s, 0], w_ss.at[s, 0])
        wait_for(wf.at[s, 0], w_ss.at[s, 1])
        for n in (2, 3):
            wait_for(wf.at[s, 0, pl.ds(0, half)], w_ss.at[s, n])
        for n in (0, 1):
            wait_for(rs1.at[s, n], g_ss.at[s, n])
            wait_for(rs2.at[s, n], g_ss.at[s, 2 + n])
        pltpu.make_async_copy(dxs.at[s, me], place(s, me), own_sem.at[2 * slots + 1 + s]).wait()
        wait_for(dxs.at[s, pl.ds(0, others)], dx_ss.at[s])
        wait_for(dxs.at[s, pl.ds(0, others)], dx_rs.at[s])


def exchange(n_dp, n_exp, send, q_send, w, x, te, dev, lane, probs):
    slots, _, depth, slabs, _ = send.shape
    cap = depth // 2
    rows = cap * n_exp
    quarter, wide = w.shape[1:]
    half = quarter // 2
    ff = wide // 3
    tokens = x.shape[0]
    vmem = pl.BlockSpec(memory_space=pltpu.VMEM)
    hbm = pl.BlockSpec(memory_space=pl.ANY)
    dma = pltpu.SemaphoreType.DMA
    return pl.pallas_call(
        functools.partial(exchange_kernel, n_dp, n_exp),
        out_shape=(
            jax.ShapeDtypeStruct((slots * rows + 1, slabs, LANES), BF16),
            jax.ShapeDtypeStruct((slots, quarter, wide), F32),
            jax.ShapeDtypeStruct((tokens, n_exp), BF16),
            jax.ShapeDtypeStruct((slabs, LANES), F32),
        ),
        in_specs=[hbm, vmem, hbm, vmem, vmem, vmem, vmem, vmem],
        out_specs=(hbm, vmem, vmem, vmem),
        scratch_shapes=[
            pltpu.VMEM(send.shape, BF16),
            pltpu.VMEM((n_exp, 1, LANES), F32),
            pltpu.VMEM((slots, n_dp, quarter, wide), BF16),
            pltpu.VMEM((rows * slabs, LANES), F32),
            pltpu.VMEM((n_dp, rows, quarter), BF16),
            pltpu.VMEM((n_dp, rows, quarter), BF16),
            pltpu.VMEM((rows, 2 * ff), BF16),
            pltpu.VMEM((rows, ff), BF16),
            pltpu.VMEM((slots, n_dp, quarter, wide), BF16),
            pltpu.VMEM((slots, 2, half, wide), BF16),
            pltpu.VMEM((slots, 2, quarter, wide), BF16),
            pltpu.VMEM((slots, n_exp, cap, slabs, LANES), BF16),
            pltpu.VMEM((slabs, LANES), BF16),
            pltpu.VMEM((n_exp, 1, LANES), F32),
            pltpu.VMEM((n_exp, 1, LANES), F32),
            pltpu.VMEM((n_exp, slabs, LANES), BF16),
            pltpu.VMEM((n_exp, slabs, LANES), BF16),
            pltpu.VMEM((n_dp, slabs, LANES), F32),
            dma((slots,)),
            dma((slots,)),
            dma,
            dma,
            dma((slots, 4)),
            dma((slots, 4)),
            dma((slots, 4)),
            dma((slots, 4)),
            dma((slots,)),
            dma((slots,)),
            dma,
            dma,
            dma,
            dma,
            dma((n_dp - 1,)),
            dma((n_dp - 1,)),
            dma((3 * slots + 1,)),
        ],
        compiler_params=pltpu.CompilerParams(
            collective_id=0, has_side_effects=True, vmem_limit_bytes=60 * 1024 * 1024
        ),
    )(send, q_send, w, x, te, dev, lane, probs)


def shards(
    n_dp,
    n_exp,
    layer_inputs,
    output_adjoint,
    dispatcher_projection,
    gating_kernel,
    expansion_kernel,
    contraction_kernel,
    token_experts,
    copy_choice_index,
    expert_copies,
    send_quotas,
):
    tokens, width = layer_inputs.shape
    fanout = token_experts.shape[1]
    experts = dispatcher_projection.shape[1]
    replicas = expert_copies.shape[1]
    position_count = send_quotas.shape[0]
    slots = gating_kernel.shape[1]
    hidden = gating_kernel.shape[2]
    slabs = width // LANES
    pairs = tokens * fanout
    sent = slots * n_exp * CAP

    logits = jnp.dot(layer_inputs, dispatcher_projection, preferred_element_type=F32)
    route_hit = token_experts[:, :, None] == lax.iota(jnp.int32, experts)[None, None, :]
    chosen = jnp.sum(jnp.where(route_hit, logits[:, None, :], 0.0), axis=2)
    probs = jax.nn.softmax(chosen, axis=1)
    flat_pick = (token_experts * replicas + copy_choice_index).reshape(pairs)
    target = jnp.sum(
        jnp.where(
            flat_pick[:, None] == lax.iota(jnp.int32, experts * replicas)[None, :],
            expert_copies.reshape(experts * replicas)[None, :],
            0,
        ),
        axis=1,
    )
    agrees = (target[:, None] == lax.iota(jnp.int32, position_count)[None, :]).astype(jnp.int32)
    arrival = jnp.sum((jnp.cumsum(agrees, axis=0) - agrees) * agrees, axis=1)
    bound = jnp.sum(agrees * send_quotas[None, :], axis=1)
    kept = arrival < bound
    owner = target // slots
    local = target % slots
    position = jnp.where(kept, (local * n_exp + owner) * CAP + arrival, sent)
    hit = position[None, :] == lax.iota(jnp.int32, sent)[:, None]
    pair_token = lax.iota(jnp.int32, pairs) // fanout
    pick = tokens - jnp.sum(jnp.where(hit, tokens - pair_token[None, :], 0), axis=1)
    sent_prob = probs.astype(BF16).astype(F32).reshape(1, pairs)
    prob = jnp.sum(jnp.where(hit, sent_prob, 0.0), axis=1).reshape(slots, n_exp, CAP)
    q_send = jnp.pad(
        prob.transpose(1, 0, 2).reshape(n_exp, 1, slots * CAP),
        ((0, 0), (0, 0), (0, LANES - slots * CAP)),
    )

    send = pl.pallas_call(
        dispatch_kernel,
        out_shape=jax.ShapeDtypeStruct((slots, n_exp, 2 * CAP, slabs, LANES), BF16),
        in_specs=[
            pl.BlockSpec(memory_space=pltpu.SMEM),
            pl.BlockSpec(memory_space=pltpu.VMEM),
            pl.BlockSpec(memory_space=pltpu.VMEM),
        ],
        out_specs=pl.BlockSpec(memory_space=pltpu.VMEM),
        scratch_shapes=[pltpu.VMEM(((tokens + 1) * slabs, LANES), F32)],
        compiler_params=pltpu.CompilerParams(vmem_limit_bytes=40 * 1024 * 1024),
    )(pick, layer_inputs, output_adjoint)

    weights = jnp.concatenate(
        [gating_kernel, expansion_kernel, contraction_kernel], axis=2
    ).transpose(1, 0, 2)
    device = jnp.where(kept, owner, -1).reshape(tokens, fanout)
    lane = (local * CAP + arrival).reshape(tokens, fanout)
    back, dw, logit_grad, router = exchange(
        n_dp,
        n_exp,
        send,
        q_send,
        weights,
        layer_inputs,
        token_experts,
        device,
        lane,
        probs,
    )
    token_grad = pl.pallas_call(
        combine_kernel,
        out_shape=jax.ShapeDtypeStruct((tokens, width), BF16),
        in_specs=[
            pl.BlockSpec(memory_space=pltpu.SMEM),
            pl.BlockSpec(memory_space=pltpu.VMEM),
            pl.BlockSpec(memory_space=pltpu.VMEM),
            pl.BlockSpec(memory_space=pltpu.VMEM),
        ],
        out_specs=pl.BlockSpec(memory_space=pltpu.VMEM),
        scratch_shapes=[pltpu.VMEM((tokens * slabs, LANES), F32)],
        compiler_params=pltpu.CompilerParams(vmem_limit_bytes=40 * 1024 * 1024),
    )(position, back, logit_grad, dispatcher_projection)

    dw = dw.transpose(1, 0, 2)
    gate_grad = dw[:, :, :hidden]
    up_grad = dw[:, :, hidden : 2 * hidden]
    down_grad = dw[:, :, 2 * hidden :]
    share = width // n_dp
    router_grad = lax.dynamic_slice(
        router.reshape(width), (lax.axis_index("dp") * share,), (share,)
    )[:, None]
    return (token_grad, gate_grad, up_grad, down_grad, router_grad)


def solution(mesh):
    return jax.shard_map(
        functools.partial(shards, mesh.shape["dp"], mesh.shape["expert"]),
        mesh=mesh,
        in_specs=(
            P(("dp", "expert"), None),
            P(("dp", "expert"), None),
            P(),
            P("dp", "expert", None),
            P("dp", "expert", None),
            P("dp", "expert", None),
            P(("dp", "expert"), None),
            P(("dp", "expert"), None),
            P(),
            P(),
        ),
        out_specs=(
            P(("dp", "expert"), None),
            P("dp", "expert", None),
            P("dp", "expert", None),
            P("dp", "expert", None),
            P("dp", "expert"),
        ),
        check_vma=False,
    )
```

```python
import functools

import jax
import jax.numpy as jnp
from jax import lax
from jax.experimental import pallas as pl
from jax.experimental.pallas import tpu as pltpu
from jax.sharding import PartitionSpec as P

CAP = 5
PLANE = 8
LANES = 128
MESH = pl.DeviceIdType.MESH
F32 = jnp.float32
BF16 = jnp.bfloat16


def slab_kernel(x_ref, g_ref, out_ref, flat):
    tokens, width = x_ref.shape
    slabs = width // LANES
    for which, ref in enumerate((x_ref, g_ref)):
        for a in range(slabs):
            flat[pl.ds(a, tokens, stride=slabs), :] = ref[:, a * LANES : (a + 1) * LANES].astype(F32)
        out_ref[which * tokens : (which + 1) * tokens] = (
            flat[...].astype(BF16).reshape(tokens, slabs, LANES)
        )
    out_ref[2 * tokens] = jnp.zeros((slabs, LANES), BF16)


def combine_kernel(place, back_ref, lg_ref, proj_ref, out_ref, flat):
    tokens, width = out_ref.shape
    slabs = width // LANES
    fanout = place.shape[0] // tokens

    def one(t, carry):
        total = back_ref[place[t * fanout]].astype(F32)
        for k in range(1, fanout):
            total = total + back_ref[place[t * fanout + k]].astype(F32)
        flat[pl.ds(pl.multiple_of(t * slabs, slabs), slabs), :] = total
        return carry

    lax.fori_loop(0, tokens, one, 0)
    for a in range(slabs):
        cols = slice(a * LANES, (a + 1) * LANES)
        routed = lax.dot_general(
            lg_ref[...], proj_ref[cols, :], (((1,), (1,)), ((), ())), preferred_element_type=F32
        )
        out_ref[:, cols] = (flat[pl.ds(a, tokens, stride=slabs), :] + routed).astype(BF16)


def exchange_kernel(
    n_dp,
    n_exp,
    block,
    table,
    q_send,
    w,
    x,
    te,
    dev,
    lane,
    probs,
    back,
    dw,
    lg_out,
    rcol,
    recv,
    sb,
    table_recv,
    table_smem,
    q_recv,
    wf,
    flat,
    xm,
    gm,
    gu,
    act_s,
    dwp,
    rs1,
    rs2,
    zero,
    pg,
    pg_recv,
    rt,
    rt_recv,
    r2,
    ring_ss,
    ring_rs,
    table_ss,
    table_rs,
    tok_ss,
    tok_rs,
    q_ss,
    q_rs,
    w_ss,
    w_rs,
    g_ss,
    g_rs,
    dx_ss,
    dx_rs,
    pg_ss,
    pg_rs,
    rt_ss,
    rt_rs,
    r2_ss,
    r2_rs,
    own_sem,
    *blocks,
):
    me = lax.axis_index("expert")
    my = lax.axis_index("dp")
    right = lax.rem(my + 1, n_dp)
    far = lax.rem(my + 2, n_dp)
    left = lax.rem(my + 3, n_dp)
    n_z, plane, depth, slabs, _ = sb.shape
    slots = w.shape[0]
    cap = depth // (2 * slots)
    rows = cap * n_exp
    tokens = x.shape[0]
    z, inner = lax.div(me, plane), lax.rem(me, plane)
    above, below = lax.rem(me + plane, n_exp), lax.rem(me + n_exp - plane, n_exp)
    quarter = wf.shape[2]
    half = quarter // 2
    ff = wf.shape[3] // 3
    per = slabs // n_dp
    chunk = plane
    others = n_exp - 1

    barrier = pltpu.get_barrier_semaphore()

    def greet(i, carry):
        pl.semaphore_signal(
            barrier, inc=1, device_id={"expert": lax.rem(me + i, n_exp)}, device_id_type=MESH
        )
        return carry

    lax.fori_loop(1, n_exp, greet, 0)
    for other in (right, far, left):
        pl.semaphore_signal(barrier, inc=1, device_id={"dp": other}, device_id_type=MESH)
    pl.semaphore_wait(barrier, others + n_dp - 1)

    def to_dp(src, dst, ss, rs, other):
        return pltpu.make_async_remote_copy(
            src, dst, ss, rs, device_id={"dp": other}, device_id_type=MESH
        )

    def to_exp(src, dst, ss, rs, other):
        return pltpu.make_async_remote_copy(
            src, dst, ss, rs, device_id={"expert": other}, device_id_type=MESH
        )

    def to_all(make):
        def one(i, carry):
            make(lax.rem(me + i, n_exp)).start()
            return carry

        lax.fori_loop(1, n_exp, one, 0)

    def wait_for(ref, sem):
        pltpu.make_async_copy(ref, ref, sem).wait()

    def w_first(s):
        for n, other in enumerate((right, left)):
            to_dp(w.at[s], wf.at[s, my], w_ss.at[s, n], w_rs.at[s, n], other).start()

    def w_second(s):
        wait_for(wf.at[s, left], w_rs.at[s, 0])
        part = wf.at[s, left, pl.ds(0, half)]
        to_dp(part, part, w_ss.at[s, 2], w_rs.at[s, 2], right).start()
        wait_for(wf.at[s, right], w_rs.at[s, 1])
        part = wf.at[s, right, pl.ds(half, half)]
        to_dp(part, part, w_ss.at[s, 3], w_rs.at[s, 3], left).start()

    def w_end(s):
        wait_for(wf.at[s, far, pl.ds(0, half)], w_rs.at[s, 2])
        wait_for(wf.at[s, far, pl.ds(half, half)], w_rs.at[s, 3])

    whole, x_part, g_part = pl.ds(0, 2 * tokens), pl.ds(0, tokens), pl.ds(tokens, tokens)
    steps = n_z // 2
    up = [block] + list(blocks[: steps - 1])
    down = [block] + list(blocks[steps - 1 : 2 * steps - 2])
    opposite = blocks[2 * steps - 2]

    def ring(t):
        last = t == steps - 1
        for n, (held, other, part) in enumerate(((up, above, x_part), (down, below, g_part))):
            part = part if last else whole
            target = opposite if last else held[t + 1]
            to_exp(
                held[t].at[part], target.at[part], ring_ss.at[n, t], ring_rs.at[n, t], other
            ).start()

    def ring_wait(t):
        last = t == steps - 1
        for n, (held, part) in enumerate(((up, x_part), (down, g_part))):
            target = opposite if last else held[t + 1]
            wait_for(target.at[part if last else whole], ring_rs.at[n, t])

    def share(rel, held):
        source = lax.rem(z + rel, n_z) * plane + inner

        def one(d, carry):
            for s in range(slots):
                for c in range(cap):
                    token = table_smem[rel, 0, (d * slots + s) * cap + c]
                    other = jnp.minimum(token + tokens, 2 * tokens)
                    sb[rel, d, s * 2 * cap + c] = held[token]
                    sb[rel, d, s * 2 * cap + cap + c] = held[other]
            return carry

        lax.fori_loop(0, plane, one, 0)

        def out(i, carry):
            d = lax.rem(inner + i, plane)
            to_exp(sb.at[rel, d], recv.at[source], tok_ss, tok_rs, z * plane + d).start()
            return carry

        lax.fori_loop(1, plane, out, 0)
        recv[source] = sb[rel, inner]

    ring(0)
    w_first(0)
    for rel in range(1, n_z):
        to_exp(
            table.at[lax.rem(z + rel, n_z)],
            table_recv.at[n_z - rel],
            table_ss,
            table_rs,
            lax.rem(me + rel * plane, n_exp),
        ).start()
    table_recv[0] = table[z]
    own = [pltpu.make_async_copy(w.at[s], wf.at[s, my], own_sem.at[s]) for s in range(slots)]
    for copy in own:
        copy.start()
    to_all(lambda d: to_exp(q_send.at[d], q_recv.at[me], q_ss, q_rs, d))
    q_recv[me] = q_send[me]
    zero[...] = jnp.zeros_like(zero)
    zero_copy = pltpu.make_async_copy(zero, back.at[slots * rows], own_sem.at[2 * slots])
    zero_copy.start()
    for held in blocks:
        held[2 * tokens] = jnp.zeros((slabs, LANES), BF16)
    wait_for(table_recv.at[pl.ds(0, n_z - 1)], table_rs)
    to_smem = pltpu.make_async_copy(table_recv, table_smem, own_sem.at[slots])
    to_smem.start()
    to_smem.wait()
    share(0, block)
    for t in range(steps - 1):
        ring_wait(t)
        ring(t + 1)
        if t == 0:
            w_second(0)
            w_first(1)
        if t == steps - 2:
            w_second(1)
        share(n_z - t - 1, up[t + 1])
        share(t + 1, down[t + 1])
    ring_wait(steps - 1)
    share(steps, opposite)

    def to_matrix(s, which, out):
        def unpack(i, carry):
            first = (2 * s + which) * cap
            part = recv[pl.ds(i * chunk, chunk), first : first + cap]
            size = chunk * cap * slabs
            flat[pl.ds(pl.multiple_of(i * size, size), size), :] = part.astype(F32).reshape(
                size, LANES
            )
            return carry

        lax.fori_loop(0, n_exp // chunk, unpack, 0)

        def gather(p, carry):
            for b in range(per):
                for c in range(cap):
                    part = flat[pl.ds(c * slabs + p * per + b, n_exp, stride=cap * slabs), :]
                    out[p, c * n_exp : (c + 1) * n_exp, b * LANES : (b + 1) * LANES] = part.astype(
                        BF16
                    )
            return carry

        lax.fori_loop(0, n_dp, gather, 0)

    lanes = lax.broadcasted_iota(jnp.int32, (n_exp, LANES), 1)

    def weight_of(s):
        table = q_recv[...].reshape(n_exp, LANES)
        return jnp.concatenate(
            [table[:, s * cap + c : s * cap + c + 1] for c in range(cap)], axis=0
        )

    def forward(s):
        to_matrix(s, 0, xm)
        to_matrix(s, 1, gm)

        def project(p, carry):
            gate_up, down = carry
            gate_up = gate_up + jnp.dot(
                xm[p], wf[s, p, :, : 2 * ff], preferred_element_type=F32
            )
            down = down + jnp.dot(gm[p], wf[s, p, :, 2 * ff :], preferred_element_type=F32)
            return gate_up, down

        gate_up, down = lax.fori_loop(
            0, n_dp, project, (jnp.zeros((rows, 2 * ff), F32), jnp.zeros((rows, ff), F32))
        )
        gate, up = gate_up[:, :ff], gate_up[:, ff:]
        sig = jax.nn.sigmoid(gate)
        silu = gate * sig
        act = (silu * up).astype(BF16)
        act_s[...] = act
        grad = jnp.sum(act.astype(F32) * down, axis=1, keepdims=True).astype(BF16).astype(F32)
        act_grad = weight_of(s) * down
        gu[:, :ff] = (act_grad * up * sig * (1.0 + gate * (1.0 - sig))).astype(BF16)
        gu[:, ff:] = (act_grad * silu).astype(BF16)
        table = jnp.zeros((n_exp, LANES), F32)
        for c in range(cap):
            table = jnp.where(
                lanes == s * cap + c, grad[c * n_exp : (c + 1) * n_exp], table
            )
        return table

    def weight_grad(s, p):
        both = (((0,), (0,)), ((), ()))
        dwp[s, p, :, : 2 * ff] = lax.dot_general(
            xm[p], gu[...], both, preferred_element_type=F32
        ).astype(BF16)
        out_grad = (weight_of(s) * gm[p].astype(F32)).astype(BF16)
        dwp[s, p, :, 2 * ff :] = lax.dot_general(
            out_grad, act_s[...], both, preferred_element_type=F32
        ).astype(BF16)

    def input_grad(s):
        def one(p, carry):
            value = lax.dot_general(
                gu[...],
                wf[s, p, :, : 2 * ff],
                (((1,), (1,)), ((), ())),
                preferred_element_type=F32,
            )
            for b in range(per):
                for c in range(cap):
                    flat[pl.ds(c * slabs + p * per + b, n_exp, stride=cap * slabs), :] = value[
                        c * n_exp : (c + 1) * n_exp, b * LANES : (b + 1) * LANES
                    ]
            return carry

        lax.fori_loop(0, n_dp, one, 0)

        def pack(i, carry):
            size = chunk * cap * slabs
            part = flat[pl.ds(pl.multiple_of(i * size, size), size), :]
            sb[i, :, s * cap : (s + 1) * cap] = part.astype(BF16).reshape(
                chunk, cap, slabs, LANES
            )
            return carry

        lax.fori_loop(0, n_exp // chunk, pack, 0)

    def place(s, d):
        return back.at[pl.ds((s * n_exp + d) * cap, cap)]

    def dx_of(s, d):
        return sb.at[lax.div(d, plane), lax.rem(d, plane), pl.ds(s * cap, cap)]

    def dx_start(s):
        pltpu.make_async_copy(
            dx_of(s, me), place(s, me), own_sem.at[2 * slots + 1 + s]
        ).start()
        to_all(lambda d: to_exp(dx_of(s, d), place(s, me), dx_ss.at[s], dx_rs.at[s], d))

    def sum_first(s):
        to_dp(
            dwp.at[s, far, pl.ds(0, half)], rs1.at[s, 0], g_ss.at[s, 0], g_rs.at[s, 0], right
        ).start()
        to_dp(
            dwp.at[s, far, pl.ds(half, half)], rs1.at[s, 1], g_ss.at[s, 1], g_rs.at[s, 1], left
        ).start()

    def sum_second(s):
        for n, other in enumerate((right, left)):
            wait_for(rs1.at[s, n], g_rs.at[s, n])
            part = pl.ds(n * half, half)
            dwp[s, other, part] = (
                dwp[s, other, part].astype(F32) + rs1[s, n].astype(F32)
            ).astype(BF16)
            to_dp(
                dwp.at[s, other], rs2.at[s, n], g_ss.at[s, 2 + n], g_rs.at[s, 2 + n], other
            ).start()

    def sum_end(s):
        wait_for(rs2.at[s, 0], g_rs.at[s, 2])
        wait_for(rs2.at[s, 1], g_rs.at[s, 3])
        dw[s] = dwp[s, my].astype(F32) + rs2[s, 0].astype(F32) + rs2[s, 1].astype(F32)

    wait_for(recv.at[pl.ds(0, n_z * (plane - 1))], tok_rs)
    wait_for(q_recv.at[pl.ds(0, others)], q_rs)
    own[0].wait()
    w_end(0)
    grads = forward(0)
    weight_grad(0, far)
    sum_first(0)
    weight_grad(0, right)
    weight_grad(0, left)
    weight_grad(0, my)
    wait_for(recv.at[pl.ds(0, n_z * (plane - 1))], tok_ss)
    input_grad(0)
    dx_start(0)
    own[1].wait()
    w_end(1)
    sum_second(0)
    grads = grads + forward(1)
    pg[...] = grads.reshape(pg.shape)
    to_all(lambda d: to_exp(pg.at[d], pg_recv.at[me], pg_ss, pg_rs, d))
    pg_recv[me] = pg[me]
    weight_grad(1, far)
    sum_first(1)
    weight_grad(1, right)
    weight_grad(1, left)
    weight_grad(1, my)
    input_grad(1)
    dx_start(1)
    sum_second(1)

    wait_for(pg_recv.at[pl.ds(0, others)], pg_rs)
    grads = pg_recv[...].reshape(n_exp, LANES).astype(BF16)
    fanout = te.shape[1]
    dev_ids = lax.broadcasted_iota(jnp.int32, (tokens, n_exp), 1)
    lane_ids = lax.broadcasted_iota(jnp.int32, (tokens, LANES), 1)
    pair = []
    weighted = jnp.zeros((tokens, 1), F32)
    for k in range(fanout):
        hit = (dev[:, k : k + 1] == dev_ids).astype(F32).astype(BF16)
        spread = jnp.dot(hit, grads, preferred_element_type=F32)
        value = jnp.sum(
            jnp.where(lane[:, k : k + 1] == lane_ids, spread, 0.0), axis=1, keepdims=True
        )
        pair.append(value)
        weighted = weighted + probs[:, k : k + 1] * value
    logit = jnp.zeros((tokens, n_exp), F32)
    for k in range(fanout):
        chosen = probs[:, k : k + 1] * (pair[k] - weighted)
        logit = logit + jnp.where(te[:, k : k + 1] == dev_ids, chosen, 0.0)
    logit = logit.astype(BF16)
    lg_out[...] = logit
    for a in range(slabs):
        flat[pl.ds(a, n_exp, stride=slabs), :] = lax.dot_general(
            logit,
            x[:, a * LANES : (a + 1) * LANES],
            (((0,), (0,)), ((), ())),
            preferred_element_type=F32,
        )
    rt[...] = flat[pl.ds(0, n_exp * slabs), :].astype(BF16).reshape(rt.shape)
    to_all(lambda d: to_exp(rt.at[d], rt_recv.at[me], rt_ss, rt_rs, d))
    rt_recv[me] = rt[me]
    sum_end(0)
    wait_for(rt_recv.at[pl.ds(0, others)], rt_rs)
    r2[0] = jnp.sum(rt_recv[...].astype(F32), axis=0)
    for n, other in enumerate((right, far, left)):
        to_dp(r2.at[0], r2.at[n + 1], r2_ss.at[n], r2_rs.at[n], other).start()
    for n in range(n_dp - 1):
        wait_for(r2.at[n + 1], r2_rs.at[n])
    rcol[...] = r2[0] + r2[1] + r2[2] + r2[3]
    sum_end(1)

    zero_copy.wait()
    wait_for(q_send.at[pl.ds(0, others)], q_ss)
    wait_for(pg.at[pl.ds(0, others)], pg_ss)
    wait_for(rt.at[pl.ds(0, others)], rt_ss)
    for n in range(n_dp - 1):
        wait_for(r2.at[0], r2_ss.at[n])
    wait_for(table.at[pl.ds(0, n_z - 1)], table_ss)
    for n, part in enumerate((x_part, g_part)):
        for t in range(steps):
            wait_for(block.at[part if t == steps - 1 else whole], ring_ss.at[n, t])
    for s in range(slots):
        wait_for(wf.at[s, 0], w_ss.at[s, 0])
        wait_for(wf.at[s, 0], w_ss.at[s, 1])
        for n in (2, 3):
            wait_for(wf.at[s, 0, pl.ds(0, half)], w_ss.at[s, n])
        for n in (0, 1):
            wait_for(rs1.at[s, n], g_ss.at[s, n])
            wait_for(rs2.at[s, n], g_ss.at[s, 2 + n])
        pltpu.make_async_copy(
            dx_of(s, me), place(s, me), own_sem.at[2 * slots + 1 + s]
        ).wait()
        wait_for(back.at[pl.ds(0, others * cap)], dx_ss.at[s])
        wait_for(back.at[pl.ds(0, others * cap)], dx_rs.at[s])


def exchange(n_dp, n_exp, block, table, q_send, w, x, te, dev, lane, probs):
    slots = w.shape[0]
    cap = CAP
    slabs = block.shape[1]
    n_z = table.shape[0]
    plane = n_exp // n_z
    rows = cap * n_exp
    quarter, wide = w.shape[1:]
    half = quarter // 2
    ff = wide // 3
    tokens = x.shape[0]
    vmem = pl.BlockSpec(memory_space=pltpu.VMEM)
    hbm = pl.BlockSpec(memory_space=pl.ANY)
    dma = pltpu.SemaphoreType.DMA
    return pl.pallas_call(
        functools.partial(exchange_kernel, n_dp, n_exp),
        out_shape=(
            jax.ShapeDtypeStruct((slots * rows + 1, slabs, LANES), BF16),
            jax.ShapeDtypeStruct((slots, quarter, wide), F32),
            jax.ShapeDtypeStruct((tokens, n_exp), BF16),
            jax.ShapeDtypeStruct((slabs, LANES), F32),
        ),
        in_specs=[vmem, vmem, vmem, hbm, vmem, vmem, vmem, vmem, vmem],
        out_specs=(hbm, vmem, vmem, vmem),
        scratch_shapes=[
            pltpu.VMEM((n_exp, 2 * slots * cap, slabs, LANES), BF16),
            pltpu.VMEM((n_z, plane, 2 * slots * cap, slabs, LANES), BF16),
            pltpu.VMEM((n_z, 1, LANES), jnp.int32),
            pltpu.SMEM((n_z, 1, LANES), jnp.int32),
            pltpu.VMEM((n_exp, 1, LANES), F32),
            pltpu.VMEM((slots, n_dp, quarter, wide), BF16),
            pltpu.VMEM((rows * slabs, LANES), F32),
            pltpu.VMEM((n_dp, rows, quarter), BF16),
            pltpu.VMEM((n_dp, rows, quarter), BF16),
            pltpu.VMEM((rows, 2 * ff), BF16),
            pltpu.VMEM((rows, ff), BF16),
            pltpu.VMEM((slots, n_dp, quarter, wide), BF16),
            pltpu.VMEM((slots, 2, half, wide), BF16),
            pltpu.VMEM((slots, 2, quarter, wide), BF16),
            pltpu.VMEM((slabs, LANES), BF16),
            pltpu.VMEM((n_exp, 1, LANES), F32),
            pltpu.VMEM((n_exp, 1, LANES), F32),
            pltpu.VMEM((n_exp, slabs, LANES), BF16),
            pltpu.VMEM((n_exp, slabs, LANES), BF16),
            pltpu.VMEM((n_dp, slabs, LANES), F32),
            dma((2, n_z // 2)),
            dma((2, n_z // 2)),
            dma,
            dma,
            dma,
            dma,
            dma,
            dma,
            dma((slots, 4)),
            dma((slots, 4)),
            dma((slots, 4)),
            dma((slots, 4)),
            dma((slots,)),
            dma((slots,)),
            dma,
            dma,
            dma,
            dma,
            dma((n_dp - 1,)),
            dma((n_dp - 1,)),
            dma((3 * slots + 1,)),
        ]
        + [pltpu.VMEM(block.shape, BF16)] * (n_z - 1),
        compiler_params=pltpu.CompilerParams(
            collective_id=0, has_side_effects=True, vmem_limit_bytes=60 * 1024 * 1024
        ),
    )(block, table, q_send, w, x, te, dev, lane, probs)


def shards(
    n_dp,
    n_exp,
    layer_inputs,
    output_adjoint,
    dispatcher_projection,
    gating_kernel,
    expansion_kernel,
    contraction_kernel,
    token_experts,
    copy_choice_index,
    expert_copies,
    send_quotas,
):
    tokens, width = layer_inputs.shape
    fanout = token_experts.shape[1]
    experts = dispatcher_projection.shape[1]
    replicas = expert_copies.shape[1]
    position_count = send_quotas.shape[0]
    slots = gating_kernel.shape[1]
    hidden = gating_kernel.shape[2]
    slabs = width // LANES
    pairs = tokens * fanout
    sent = slots * n_exp * CAP

    logits = jnp.dot(layer_inputs, dispatcher_projection, preferred_element_type=F32)
    route_hit = token_experts[:, :, None] == lax.iota(jnp.int32, experts)[None, None, :]
    chosen = jnp.sum(jnp.where(route_hit, logits[:, None, :], 0.0), axis=2)
    probs = jax.nn.softmax(chosen, axis=1)
    flat_pick = (token_experts * replicas + copy_choice_index).reshape(pairs)
    target = jnp.sum(
        jnp.where(
            flat_pick[:, None] == lax.iota(jnp.int32, experts * replicas)[None, :],
            expert_copies.reshape(experts * replicas)[None, :],
            0,
        ),
        axis=1,
    )
    agrees = (target[:, None] == lax.iota(jnp.int32, position_count)[None, :]).astype(jnp.int32)
    arrival = jnp.sum((jnp.cumsum(agrees, axis=0) - agrees) * agrees, axis=1)
    bound = jnp.sum(agrees * send_quotas[None, :], axis=1)
    kept = arrival < bound
    owner = target // slots
    local = target % slots
    position = jnp.where(kept, (local * n_exp + owner) * CAP + arrival, sent)
    hit = position[None, :] == lax.iota(jnp.int32, sent)[:, None]
    pair_token = lax.iota(jnp.int32, pairs) // fanout
    pick = 2 * tokens - jnp.sum(jnp.where(hit, 2 * tokens - pair_token[None, :], 0), axis=1)
    sent_prob = probs.astype(BF16).astype(F32).reshape(1, pairs)
    prob = jnp.sum(jnp.where(hit, sent_prob, 0.0), axis=1).reshape(slots, n_exp, CAP)
    q_send = jnp.pad(
        prob.transpose(1, 0, 2).reshape(n_exp, 1, slots * CAP),
        ((0, 0), (0, 0), (0, LANES - slots * CAP)),
    )

    n_z = n_exp // PLANE
    table = jnp.pad(
        pick.reshape(slots, n_z, PLANE, CAP).transpose(1, 2, 0, 3).reshape(n_z, 1, slots * PLANE * CAP),
        ((0, 0), (0, 0), (0, LANES - slots * PLANE * CAP)),
    )
    block = pl.pallas_call(
        slab_kernel,
        out_shape=jax.ShapeDtypeStruct((2 * tokens + 1, slabs, LANES), BF16),
        in_specs=[pl.BlockSpec(memory_space=pltpu.VMEM)] * 2,
        out_specs=pl.BlockSpec(memory_space=pltpu.VMEM),
        scratch_shapes=[pltpu.VMEM((tokens * slabs, LANES), F32)],
        compiler_params=pltpu.CompilerParams(vmem_limit_bytes=40 * 1024 * 1024),
    )(layer_inputs, output_adjoint)

    weights = jnp.concatenate(
        [gating_kernel, expansion_kernel, contraction_kernel], axis=2
    ).transpose(1, 0, 2)
    device = jnp.where(kept, owner, -1).reshape(tokens, fanout)
    lane = (local * CAP + arrival).reshape(tokens, fanout)
    back, dw, logit_grad, router = exchange(
        n_dp,
        n_exp,
        block,
        table,
        q_send,
        weights,
        layer_inputs,
        token_experts,
        device,
        lane,
        probs,
    )
    token_grad = pl.pallas_call(
        combine_kernel,
        out_shape=jax.ShapeDtypeStruct((tokens, width), BF16),
        in_specs=[
            pl.BlockSpec(memory_space=pltpu.SMEM),
            pl.BlockSpec(memory_space=pltpu.VMEM),
            pl.BlockSpec(memory_space=pltpu.VMEM),
            pl.BlockSpec(memory_space=pltpu.VMEM),
        ],
        out_specs=pl.BlockSpec(memory_space=pltpu.VMEM),
        scratch_shapes=[pltpu.VMEM((tokens * slabs, LANES), F32)],
        compiler_params=pltpu.CompilerParams(vmem_limit_bytes=40 * 1024 * 1024),
    )(position, back, logit_grad, dispatcher_projection)

    dw = dw.transpose(1, 0, 2)
    gate_grad = dw[:, :, :hidden]
    up_grad = dw[:, :, hidden : 2 * hidden]
    down_grad = dw[:, :, 2 * hidden :]
    share = width // n_dp
    router_grad = lax.dynamic_slice(
        router.reshape(width), (lax.axis_index("dp") * share,), (share,)
    )[:, None]
    return (token_grad, gate_grad, up_grad, down_grad, router_grad)


def solution(mesh):
    return jax.shard_map(
        functools.partial(shards, mesh.shape["dp"], mesh.shape["expert"]),
        mesh=mesh,
        in_specs=(
            P(("dp", "expert"), None),
            P(("dp", "expert"), None),
            P(),
            P("dp", "expert", None),
            P("dp", "expert", None),
            P("dp", "expert", None),
            P(("dp", "expert"), None),
            P(("dp", "expert"), None),
            P(),
            P(),
        ),
        out_specs=(
            P(("dp", "expert"), None),
            P("dp", "expert", None),
            P("dp", "expert", None),
            P("dp", "expert", None),
            P("dp", "expert"),
        ),
        check_vma=False,
    )
```

```python
import functools

import jax
import jax.numpy as jnp
from jax import lax
from jax.experimental import pallas as pl
from jax.experimental.pallas import tpu as pltpu
from jax.sharding import PartitionSpec as P

CAP = 5
PLANE = 8
LANES = 128
MESH = pl.DeviceIdType.MESH
F32 = jnp.float32
BF16 = jnp.bfloat16


def slab_kernel(x_ref, g_ref, out_ref, flat):
    tokens, width = x_ref.shape
    slabs = width // LANES
    for which, ref in enumerate((x_ref, g_ref)):
        for a in range(slabs):
            flat[pl.ds(a, tokens, stride=slabs), :] = ref[:, a * LANES : (a + 1) * LANES].astype(F32)
        out_ref[which * tokens : (which + 1) * tokens] = (
            flat[...].astype(BF16).reshape(tokens, slabs, LANES)
        )
    out_ref[2 * tokens] = jnp.zeros((slabs, LANES), BF16)


def exchange_kernel(
    n_dp,
    n_exp,
    place,
    block,
    table,
    q_table,
    w,
    x,
    proj,
    te,
    dev,
    lane,
    probs,
    token_grad,
    dw,
    rcol,
    recv,
    sb,
    dxs,
    back,
    table_recv,
    table_smem,
    q_mid,
    q_all,
    wf,
    flat,
    xm,
    gm,
    gu,
    act_s,
    q_col,
    dwp,
    from_mate,
    from_mate2,
    from_partner,
    pg,
    pg_recv,
    rt,
    rt_recv,
    r2,
    sums,
    ring_ss,
    ring_rs,
    table_ss,
    table_rs,
    qt_ss,
    qt_rs,
    q_ss,
    q_rs,
    tok_ss,
    tok_rs,
    w_ss,
    w_rs,
    g_ss,
    g_rs,
    dx_ss,
    dx_rs,
    pg_ss,
    pg_rs,
    rt_ss,
    rt_rs,
    r2_ss,
    r2_rs,
    own_sem,
    *blocks,
):
    me = lax.axis_index("expert")
    my = lax.axis_index("dp")
    partner = n_dp - 1 - my
    slot = lax.div(my, 2)
    other_slot = 1 - slot
    mate = my + 1 - 2 * lax.rem(my, 2)
    corner = n_dp - 1 - mate
    n_z, sides, depth, slabs, _ = sb.shape
    plane = sides // 2
    cap = depth // 2
    group = sides * cap
    rows = n_z * group
    tokens = x.shape[0]
    z, inner = lax.div(me, plane), lax.rem(me, plane)
    above, below = lax.rem(me + plane, n_exp), lax.rem(me + n_exp - plane, n_exp)
    quarter = wf.shape[1]
    half = quarter // 2
    ff = wf.shape[2] // 3
    per = slabs // n_dp
    others = n_exp - 1

    barrier = pltpu.get_barrier_semaphore()

    def greet(d, e):
        pl.semaphore_signal(
            barrier, inc=1, device_id={"dp": d, "expert": e}, device_id_type=MESH
        )

    def greet_both(i, carry):
        greet(my, lax.rem(me + i, n_exp))
        greet(partner, lax.rem(me + i, n_exp))
        return carry

    greet(mate, me)
    greet(corner, me)
    greet(partner, me)
    lax.fori_loop(1, n_exp, greet_both, 0)
    pl.semaphore_wait(barrier, 2 * n_exp + 1)

    def to(src, dst, ss, rs, d, e):
        return pltpu.make_async_remote_copy(
            src, dst, ss, rs, device_id={"dp": d, "expert": e}, device_id_type=MESH
        )

    def wait_for(ref, sem):
        pltpu.make_async_copy(ref, ref, sem).wait()

    whole, x_part, g_part = pl.ds(0, 2 * tokens), pl.ds(0, tokens), pl.ds(tokens, tokens)
    steps = n_z // 2
    up = [block] + list(blocks[: steps - 1])
    down = [block] + list(blocks[steps - 1 : 2 * steps - 2])
    opposite = blocks[2 * steps - 2]

    def ring(t):
        last = t == steps - 1
        for n, (held, e, part) in enumerate(((up, above, x_part), (down, below, g_part))):
            part = part if last else whole
            target = opposite if last else held[t + 1]
            to(
                held[t].at[part], target.at[part], ring_ss.at[n, t], ring_rs.at[n, t], my, e
            ).start()

    def ring_wait(t):
        last = t == steps - 1
        for n, (held, part) in enumerate(((up, x_part), (down, g_part))):
            target = opposite if last else held[t + 1]
            wait_for(target.at[part if last else whole], ring_rs.at[n, t])

    def share(rel, held):
        def one(d, carry):
            for side, s in enumerate((slot, other_slot)):
                first = (2 * d + s) * cap
                for c in range(cap):
                    token = table_smem[rel, 0, first + c]
                    sb[rel, side * plane + d, c] = held[token]
                    sb[rel, side * plane + d, cap + c] = held[
                        jnp.minimum(token + tokens, 2 * tokens)
                    ]
            return carry

        lax.fori_loop(0, plane, one, 0)

        def out(i, carry):
            d = lax.rem(inner + i, plane)
            for side, y in enumerate((my, partner)):
                to(
                    sb.at[rel, side * plane + d],
                    recv.at[rel, side * plane + inner],
                    tok_ss,
                    tok_rs.at[rel],
                    y,
                    z * plane + d,
                ).start()
            return carry

        to(
            sb.at[rel, plane + inner],
            recv.at[rel, plane + inner],
            tok_ss,
            tok_rs.at[rel],
            partner,
            me,
        ).start()
        lax.fori_loop(1, plane, out, 0)
        recv[rel, inner] = sb[rel, inner]

    ring(0)
    to(w.at[slot], wf.at[my], w_ss.at[0], w_rs.at[0], mate, me).start()
    to(w.at[other_slot], wf.at[my], w_ss.at[1], w_rs.at[1], partner, me).start()
    own_w = pltpu.make_async_copy(w.at[slot], wf.at[my], own_sem.at[0])
    own_w.start()
    for source, target, ss, rs in (
        (table, table_recv, table_ss, table_rs),
        (q_table, q_mid, qt_ss, qt_rs),
    ):
        for rel in range(1, n_z):
            to(
                source.at[lax.rem(z + rel, n_z)],
                target.at[n_z - rel],
                ss,
                rs,
                my,
                lax.rem(me + rel * plane, n_exp),
            ).start()
        target[0] = source[z]
    for held in blocks:
        held[2 * tokens] = jnp.zeros((slabs, LANES), BF16)
    back[2 * n_exp * cap] = jnp.zeros((slabs, LANES), BF16)
    wait_for(table_recv.at[pl.ds(0, n_z - 1)], table_rs)
    to_smem = pltpu.make_async_copy(table_recv, table_smem, own_sem.at[1])
    to_smem.start()
    wait_for(q_mid.at[pl.ds(0, n_z - 1)], qt_rs)

    def q_out(i, carry):
        e = z * plane + lax.rem(inner + i, plane)
        for side, y in enumerate((my, partner)):
            to(q_mid, q_all.at[side * plane + inner], q_ss, q_rs, y, e).start()
        return carry

    to(q_mid, q_all.at[plane + inner], q_ss, q_rs, partner, me).start()
    lax.fori_loop(1, plane, q_out, 0)
    q_all[inner] = q_mid[...]
    to_smem.wait()

    lanes = lax.broadcasted_iota(jnp.int32, (sides, LANES), 1)

    def to_matrix(rel, which, out):
        part = recv[rel, :, which * cap : (which + 1) * cap]
        flat[...] = part.astype(F32).reshape(group * slabs, LANES)

        def gather(p, carry):
            for b in range(per):
                for c in range(cap):
                    value = flat[pl.ds(c * slabs + p * per + b, sides, stride=cap * slabs), :]
                    first = rel * group + c * sides
                    out[p, first : first + sides, b * LANES : (b + 1) * LANES] = value.astype(BF16)
            return carry

        lax.fori_loop(0, n_dp, gather, 0)

    def process(rel):
        wait_for(recv.at[rel, pl.ds(0, sides - 1)], tok_rs.at[rel])
        here = slice(rel * group, (rel + 1) * group)
        to_matrix(rel, 0, xm)
        to_matrix(rel, 1, gm)
        weights = q_all[:, rel].reshape(sides, LANES)
        weight = jnp.concatenate(
            [
                jnp.sum(
                    jnp.where(lanes == (2 * inner + slot) * cap + c, weights, 0.0),
                    axis=1,
                    keepdims=True,
                )
                for c in range(cap)
            ],
            axis=0,
        )
        q_col[here] = jnp.broadcast_to(weight, (group, LANES))

        def project(p, carry):
            gate_up, down = carry
            gate_up = gate_up + jnp.dot(
                xm[p, here], wf[p, :, : 2 * ff], preferred_element_type=F32
            )
            down = down + jnp.dot(gm[p, here], wf[p, :, 2 * ff :], preferred_element_type=F32)
            return gate_up, down

        gate_up, down = lax.fori_loop(
            0, n_dp, project, (jnp.zeros((group, 2 * ff), F32), jnp.zeros((group, ff), F32))
        )
        gate, up_value = gate_up[:, :ff], gate_up[:, ff:]
        sig = jax.nn.sigmoid(gate)
        silu = gate * sig
        act = (silu * up_value).astype(BF16)
        act_s[here] = act
        grad = jnp.sum(act.astype(F32) * down, axis=1, keepdims=True).astype(BF16).astype(F32)
        act_grad = weight * down
        gu[here, :ff] = (act_grad * up_value * sig * (1.0 + gate * (1.0 - sig))).astype(BF16)
        gu[here, ff:] = (act_grad * silu).astype(BF16)
        grads = jnp.zeros((sides, LANES), F32)
        for c in range(cap):
            grads = jnp.where(
                lanes == slot * cap + c, grad[c * sides : (c + 1) * sides], grads
            )
        pg[rel] = grads.reshape(sides, 1, LANES)

        def expand(p, carry):
            value = lax.dot_general(
                gu[here],
                wf[p, :, : 2 * ff],
                (((1,), (1,)), ((), ())),
                preferred_element_type=F32,
            )
            for b in range(per):
                for c in range(cap):
                    flat[pl.ds(c * slabs + p * per + b, sides, stride=cap * slabs), :] = value[
                        c * sides : (c + 1) * sides, b * LANES : (b + 1) * LANES
                    ]
            return carry

        lax.fori_loop(0, n_dp, expand, 0)
        dxs[rel] = flat[...].astype(BF16).reshape(sides, cap, slabs, LANES)

    def send_back(rel, source, target, ss, rs):
        first = lax.rem(z + rel, n_z) * plane

        def both(i, carry):
            d = lax.rem(inner + i, plane)
            for side, y in enumerate((my, partner)):
                to(source.at[rel, side * plane + d], target, ss, rs, y, first + d).start()
            return carry

        if rel:
            lax.fori_loop(0, plane, both, 0)
        else:
            to(source.at[rel, plane + inner], target, ss, rs, partner, me).start()
            lax.fori_loop(1, plane, both, 0)

    spot = slot * n_exp + me
    own_rows = pl.ds(spot * cap, cap)

    def pg_start(rel):
        send_back(rel, pg, pg_recv.at[spot], pg_ss, pg_rs)
        if rel == 0:
            pg_recv[spot] = pg[0, inner]

    def dx_start(rel):
        send_back(rel, dxs, back.at[own_rows], dx_ss, dx_rs)
        if rel == 0:
            back[own_rows] = dxs[0, inner]

    def weight_grad(p):
        both = (((0,), (0,)), ((), ()))
        dwp[p, :, : 2 * ff] = lax.dot_general(
            xm[p], gu[...], both, preferred_element_type=F32
        ).astype(BF16)
        out_grad = jnp.concatenate(
            [
                (q_col[...] * gm[p, :, n * LANES : (n + 1) * LANES].astype(F32)).astype(BF16)
                for n in range(quarter // LANES)
            ],
            axis=1,
        )
        dwp[p, :, 2 * ff :] = lax.dot_general(
            out_grad, act_s[...], both, preferred_element_type=F32
        ).astype(BF16)

    share(0, block)
    done = [0]
    for t in range(steps - 1):
        ring_wait(t)
        ring(t + 1)
        if t == 0:
            wait_for(wf.at[partner], w_rs.at[1])
            to(wf.at[partner], wf.at[partner], w_ss.at[2], w_rs.at[2], mate, me).start()
        share(n_z - t - 1, up[t + 1])
        share(t + 1, down[t + 1])
        if t == steps - 2:
            own_w.wait()
            wait_for(wf.at[mate], w_rs.at[0])
            wait_for(wf.at[corner], w_rs.at[2])
            wait_for(q_all.at[pl.ds(0, sides - 1)], q_rs)
            for rel in done:
                process(rel)
                pg_start(rel)
            last = (n_z - t - 1, t + 1)
        else:
            done += [n_z - t - 1, t + 1]
    ring_wait(steps - 1)
    share(steps, opposite)
    for rel in done:
        dx_start(rel)
    for rel in last:
        process(rel)
        pg_start(rel)
        dx_start(rel)
    process(steps)
    pg_start(steps)

    def give(n, source, target, d):
        to(source, target, g_ss.at[n], g_rs.at[n], d, me).start()

    weight_grad(corner)
    for n in range(2):
        part = pl.ds(n * half, half)
        give(n, dwp.at[corner, part], from_mate.at[part], mate)
    dx_start(steps)
    weight_grad(mate)
    give(2, dwp.at[mate], from_mate2, mate)
    weight_grad(partner)
    for n in range(2):
        part = pl.ds(n * half, half)
        wait_for(from_mate.at[part], g_rs.at[n])
        dwp[partner, part] = (
            dwp[partner, part].astype(F32) + from_mate[part].astype(F32)
        ).astype(BF16)
        give(3 + n, dwp.at[partner, part], from_partner.at[part], partner)
    weight_grad(my)

    wait_for(pg_recv.at[pl.ds(0, 2 * n_exp - 1)], pg_rs)
    grads = pg_recv[...].reshape(2 * n_exp, LANES)
    grads = (grads[:n_exp] + grads[n_exp:]).astype(BF16)
    fanout = te.shape[1]
    dev_ids = lax.broadcasted_iota(jnp.int32, (tokens, n_exp), 1)
    lane_ids = lax.broadcasted_iota(jnp.int32, (tokens, LANES), 1)
    pair = []
    weighted = jnp.zeros((tokens, 1), F32)
    for k in range(fanout):
        hit = (dev[:, k : k + 1] == dev_ids).astype(F32).astype(BF16)
        spread = jnp.dot(hit, grads, preferred_element_type=F32)
        value = jnp.sum(
            jnp.where(lane[:, k : k + 1] == lane_ids, spread, 0.0), axis=1, keepdims=True
        )
        pair.append(value)
        weighted = weighted + probs[:, k : k + 1] * value
    logit = jnp.zeros((tokens, n_exp), F32)
    for k in range(fanout):
        chosen = probs[:, k : k + 1] * (pair[k] - weighted)
        logit = logit + jnp.where(te[:, k : k + 1] == dev_ids, chosen, 0.0)
    logit = logit.astype(BF16)
    for a in range(slabs):
        r_cols = lax.dot_general(
            logit,
            x[:, a * LANES : (a + 1) * LANES],
            (((0,), (0,)), ((), ())),
            preferred_element_type=F32,
        )
        flat[pl.ds(a, n_exp, stride=slabs), :] = r_cols
    rt[...] = flat[pl.ds(0, n_exp * slabs), :].astype(BF16).reshape(rt.shape)

    def rt_out(i, carry):
        d = lax.rem(me + i, n_exp)
        to(rt.at[d], rt_recv.at[me], rt_ss, rt_rs, my, d).start()
        return carry

    lax.fori_loop(1, n_exp, rt_out, 0)
    rt_recv[me] = rt[me]
    wait_for(rt_recv.at[pl.ds(0, others)], rt_rs)
    r2[0] = jnp.sum(rt_recv[...].astype(F32), axis=0)
    for n, d in enumerate((mate, partner, corner)):
        to(r2.at[0], r2.at[n + 1], r2_ss.at[n], r2_rs.at[n], d, me).start()

    wait_for(back.at[pl.ds(0, (2 * n_exp - 1) * cap)], dx_rs)

    def combine(t, carry):
        total = back[place[t * fanout]].astype(F32)
        for k in range(1, fanout):
            total = total + back[place[t * fanout + k]].astype(F32)
        sums[pl.ds(pl.multiple_of(t * slabs, slabs), slabs), :] = total
        return carry

    lax.fori_loop(0, tokens, combine, 0)
    for a in range(slabs):
        cols = slice(a * LANES, (a + 1) * LANES)
        routed = lax.dot_general(
            logit, proj[cols, :], (((1,), (1,)), ((), ())), preferred_element_type=F32
        )
        token_grad[:, cols] = (sums[pl.ds(a, tokens, stride=slabs), :] + routed).astype(BF16)

    for n in range(n_dp - 1):
        wait_for(r2.at[n + 1], r2_rs.at[n])
    rcol[...] = r2[0] + r2[1] + r2[2] + r2[3]
    for n in range(2):
        part = pl.ds(n * half, half)
        wait_for(from_partner.at[part], g_rs.at[3 + n])
    dw[other_slot] = from_partner[...].astype(F32)
    wait_for(from_mate2, g_rs.at[2])
    dw[slot] = dwp[my].astype(F32) + from_mate2[...].astype(F32)

    for n, part in enumerate((x_part, g_part)):
        for t in range(steps):
            wait_for(block.at[part if t == steps - 1 else whole], ring_ss.at[n, t])
    wait_for(table.at[pl.ds(0, n_z - 1)], table_ss)
    wait_for(q_table.at[pl.ds(0, n_z - 1)], qt_ss)
    wait_for(q_all.at[pl.ds(0, sides - 1)], q_ss)
    for rel in range(n_z):
        wait_for(recv.at[rel, pl.ds(0, sides - 1)], tok_ss)
    for n in range(3):
        wait_for(wf.at[0], w_ss.at[n])
    for n in (0, 1, 3, 4):
        wait_for(from_mate.at[pl.ds(0, half)], g_ss.at[n])
    wait_for(from_mate2, g_ss.at[2])
    wait_for(back.at[pl.ds(0, (2 * n_exp - 1) * cap)], dx_ss)
    wait_for(pg_recv.at[pl.ds(0, 2 * n_exp - 1)], pg_ss)
    wait_for(rt.at[pl.ds(0, others)], rt_ss)
    for n in range(n_dp - 1):
        wait_for(r2.at[0], r2_ss.at[n])


def exchange(n_dp, n_exp, place, block, table, q_table, w, x, proj, te, dev, lane, probs):
    slots, quarter, wide = w.shape
    cap = CAP
    slabs = block.shape[1]
    n_z = table.shape[0]
    sides = 2 * n_exp // n_z
    group = sides * cap
    rows = n_z * group
    ff = wide // 3
    tokens, width = x.shape
    vmem = pl.BlockSpec(memory_space=pltpu.VMEM)
    hbm = pl.BlockSpec(memory_space=pl.ANY)
    smem = pl.BlockSpec(memory_space=pltpu.SMEM)
    dma = pltpu.SemaphoreType.DMA
    return pl.pallas_call(
        functools.partial(exchange_kernel, n_dp, n_exp),
        out_shape=(
            jax.ShapeDtypeStruct((tokens, width), BF16),
            jax.ShapeDtypeStruct((slots, quarter, wide), F32),
            jax.ShapeDtypeStruct((slabs, LANES), F32),
        ),
        in_specs=[smem, vmem, vmem, vmem, hbm] + [vmem] * 6,
        out_specs=(vmem, vmem, vmem),
        scratch_shapes=[
            pltpu.VMEM((n_z, sides, 2 * cap, slabs, LANES), BF16),
            pltpu.VMEM((n_z, sides, 2 * cap, slabs, LANES), BF16),
            pltpu.VMEM((n_z, sides, cap, slabs, LANES), BF16),
            pltpu.VMEM((2 * n_exp * cap + 1, slabs, LANES), BF16),
            pltpu.VMEM((n_z, 1, LANES), jnp.int32),
            pltpu.SMEM((n_z, 1, LANES), jnp.int32),
            pltpu.VMEM((n_z, 1, LANES), F32),
            pltpu.VMEM((sides, n_z, 1, LANES), F32),
            pltpu.VMEM((n_dp, quarter, wide), BF16),
            pltpu.VMEM((max(group, n_exp) * slabs, LANES), F32),
            pltpu.VMEM((n_dp, rows, quarter), BF16),
            pltpu.VMEM((n_dp, rows, quarter), BF16),
            pltpu.VMEM((rows, 2 * ff), BF16),
            pltpu.VMEM((rows, ff), BF16),
            pltpu.VMEM((rows, LANES), F32),
            pltpu.VMEM((n_dp, quarter, wide), BF16),
            pltpu.VMEM((quarter, wide), BF16),
            pltpu.VMEM((quarter, wide), BF16),
            pltpu.VMEM((quarter, wide), BF16),
            pltpu.VMEM((n_z, sides, 1, LANES), F32),
            pltpu.VMEM((2 * n_exp, 1, LANES), F32),
            pltpu.VMEM((n_exp, slabs, LANES), BF16),
            pltpu.VMEM((n_exp, slabs, LANES), BF16),
            pltpu.VMEM((n_dp, slabs, LANES), F32),
            pltpu.VMEM((tokens * slabs, LANES), F32),
            dma((2, n_z // 2)),
            dma((2, n_z // 2)),
            dma,
            dma,
            dma,
            dma,
            dma,
            dma,
            dma,
            dma((n_z,)),
            dma((3,)),
            dma((3,)),
            dma((5,)),
            dma((5,)),
            dma,
            dma,
            dma,
            dma,
            dma,
            dma,
            dma((n_dp - 1,)),
            dma((n_dp - 1,)),
            dma((2,)),
        ]
        + [pltpu.VMEM(block.shape, BF16)] * (n_z - 1),
        compiler_params=pltpu.CompilerParams(
            collective_id=0, has_side_effects=True, vmem_limit_bytes=60 * 1024 * 1024
        ),
    )(place, block, table, q_table, w, x, proj, te, dev, lane, probs)


def shards(
    n_dp,
    n_exp,
    layer_inputs,
    output_adjoint,
    dispatcher_projection,
    gating_kernel,
    expansion_kernel,
    contraction_kernel,
    token_experts,
    copy_choice_index,
    expert_copies,
    send_quotas,
):
    tokens, width = layer_inputs.shape
    fanout = token_experts.shape[1]
    experts = dispatcher_projection.shape[1]
    replicas = expert_copies.shape[1]
    position_count = send_quotas.shape[0]
    slots = gating_kernel.shape[1]
    hidden = gating_kernel.shape[2]
    slabs = width // LANES
    pairs = tokens * fanout
    sent = slots * n_exp * CAP

    logits = jnp.dot(layer_inputs, dispatcher_projection, preferred_element_type=F32)
    route_hit = token_experts[:, :, None] == lax.iota(jnp.int32, experts)[None, None, :]
    chosen = jnp.sum(jnp.where(route_hit, logits[:, None, :], 0.0), axis=2)
    probs = jax.nn.softmax(chosen, axis=1)
    flat_pick = (token_experts * replicas + copy_choice_index).reshape(pairs)
    target = jnp.sum(
        jnp.where(
            flat_pick[:, None] == lax.iota(jnp.int32, experts * replicas)[None, :],
            expert_copies.reshape(experts * replicas)[None, :],
            0,
        ),
        axis=1,
    )
    agrees = (target[:, None] == lax.iota(jnp.int32, position_count)[None, :]).astype(jnp.int32)
    arrival = jnp.sum((jnp.cumsum(agrees, axis=0) - agrees) * agrees, axis=1)
    bound = jnp.sum(agrees * send_quotas[None, :], axis=1)
    kept = arrival < bound
    owner = target // slots
    local = target % slots
    position = jnp.where(kept, (local * n_exp + owner) * CAP + arrival, sent)
    hit = position[None, :] == lax.iota(jnp.int32, sent)[:, None]
    pair_token = lax.iota(jnp.int32, pairs) // fanout
    pick = 2 * tokens - jnp.sum(jnp.where(hit, 2 * tokens - pair_token[None, :], 0), axis=1)
    sent_prob = probs.astype(BF16).astype(F32).reshape(1, pairs)
    prob = jnp.sum(jnp.where(hit, sent_prob, 0.0), axis=1)
    n_z = n_exp // PLANE

    def by_plane(values):
        count = slots * PLANE * CAP
        values = values.reshape(slots, n_z, PLANE, CAP).transpose(1, 2, 0, 3)
        return jnp.pad(values.reshape(n_z, 1, count), ((0, 0), (0, 0), (0, LANES - count)))

    table, q_table = by_plane(pick), by_plane(prob)
    block = pl.pallas_call(
        slab_kernel,
        out_shape=jax.ShapeDtypeStruct((2 * tokens + 1, slabs, LANES), BF16),
        in_specs=[pl.BlockSpec(memory_space=pltpu.VMEM)] * 2,
        out_specs=pl.BlockSpec(memory_space=pltpu.VMEM),
        scratch_shapes=[pltpu.VMEM((tokens * slabs, LANES), F32)],
        compiler_params=pltpu.CompilerParams(vmem_limit_bytes=40 * 1024 * 1024),
    )(layer_inputs, output_adjoint)

    weights = jnp.concatenate(
        [gating_kernel, expansion_kernel, contraction_kernel], axis=2
    ).transpose(1, 0, 2)
    device = jnp.where(kept, owner, -1).reshape(tokens, fanout)
    lane = (local * CAP + arrival).reshape(tokens, fanout)
    token_grad, dw, router = exchange(
        n_dp,
        n_exp,
        position,
        block,
        table,
        q_table,
        weights,
        layer_inputs,
        dispatcher_projection,
        token_experts,
        device,
        lane,
        probs,
    )
    dw = dw.transpose(1, 0, 2)
    gate_grad = dw[:, :, :hidden]
    up_grad = dw[:, :, hidden : 2 * hidden]
    down_grad = dw[:, :, 2 * hidden :]
    share = width // n_dp
    router_grad = lax.dynamic_slice(
        router.reshape(width), (lax.axis_index("dp") * share,), (share,)
    )[:, None]
    return (token_grad, gate_grad, up_grad, down_grad, router_grad)


def solution(mesh):
    return jax.shard_map(
        functools.partial(shards, mesh.shape["dp"], mesh.shape["expert"]),
        mesh=mesh,
        in_specs=(
            P(("dp", "expert"), None),
            P(("dp", "expert"), None),
            P(),
            P("dp", "expert", None),
            P("dp", "expert", None),
            P("dp", "expert", None),
            P(("dp", "expert"), None),
            P(("dp", "expert"), None),
            P(),
            P(),
        ),
        out_specs=(
            P(("dp", "expert"), None),
            P("dp", "expert", None),
            P("dp", "expert", None),
            P("dp", "expert", None),
            P("dp", "expert"),
        ),
        check_vma=False,
    )
```

```python
import functools

import jax
import jax.numpy as jnp
from jax import lax
from jax.experimental import pallas as pl
from jax.experimental.pallas import tpu as pltpu
from jax.sharding import PartitionSpec as P

CAP = 5
PLANE = 8
LANES = 128
MESH = pl.DeviceIdType.MESH
F32 = jnp.float32
BF16 = jnp.bfloat16


def exchange_kernel(
    n_dp,
    n_exp,
    place,
    table,
    q_table,
    w,
    x,
    g,
    proj,
    te,
    plane_of,
    lane,
    probs,
    token_grad,
    gate_grad,
    up_grad,
    down_grad,
    rcol,
    block,
    recv,
    sb,
    dxs,
    back,
    table_recv,
    table_smem,
    q_mid,
    q_all,
    wf,
    flat,
    xm,
    gm,
    gu,
    act_s,
    q_col,
    dwp,
    from_mate,
    from_mate2,
    from_partner,
    pg,
    pg_in,
    pg_mid,
    pg_recv,
    rt,
    rt_recv,
    r2,
    sums,
    ring_ss,
    ring_rs,
    table_ss,
    table_rs,
    qt_ss,
    qt_rs,
    q_ss,
    q_rs,
    tok_ss,
    tok_rs,
    w_ss,
    w_rs,
    g_ss,
    g_rs,
    dx_ss,
    dx_rs,
    pg_ss,
    pg_rs,
    pm_ss,
    pm_rs,
    rt_ss,
    rt_rs,
    r2_ss,
    r2_rs,
    own_sem,
    *blocks,
):
    me = lax.axis_index("expert")
    my = lax.axis_index("dp")
    partner = n_dp - 1 - my
    slot = lax.div(my, 2)
    other_slot = 1 - slot
    mate = my + 1 - 2 * lax.rem(my, 2)
    corner = n_dp - 1 - mate
    n_z, sides, depth, slabs, _ = sb.shape
    plane = sides // 2
    cap = depth // 2
    group = sides * cap
    rows = n_z * group
    tokens = x.shape[0]
    z, inner = lax.div(me, plane), lax.rem(me, plane)
    above, below = lax.rem(me + plane, n_exp), lax.rem(me + n_exp - plane, n_exp)
    quarter = wf.shape[1]
    half = quarter // 2
    ff = wf.shape[2] // 3
    per = slabs // n_dp
    others = n_exp - 1

    for which, ref in enumerate((x, g)):
        for a in range(slabs):
            sums[pl.ds(a, tokens, stride=slabs), :] = ref[:, a * LANES : (a + 1) * LANES].astype(F32)
        block[which * tokens : (which + 1) * tokens] = (
            sums[...].astype(BF16).reshape(tokens, slabs, LANES)
        )
    block[2 * tokens] = jnp.zeros((slabs, LANES), BF16)

    barrier = pltpu.get_barrier_semaphore()

    def greet(d, e):
        pl.semaphore_signal(
            barrier, inc=1, device_id={"dp": d, "expert": e}, device_id_type=MESH
        )

    def greet_both(i, carry):
        greet(my, lax.rem(me + i, n_exp))
        greet(partner, lax.rem(me + i, n_exp))
        return carry

    greet(mate, me)
    greet(corner, me)
    greet(partner, me)
    lax.fori_loop(1, n_exp, greet_both, 0)
    pl.semaphore_wait(barrier, 2 * n_exp + 1)

    def to(src, dst, ss, rs, d, e):
        return pltpu.make_async_remote_copy(
            src, dst, ss, rs, device_id={"dp": d, "expert": e}, device_id_type=MESH
        )

    def wait_for(ref, sem):
        pltpu.make_async_copy(ref, ref, sem).wait()

    parts = (pl.ds(0, tokens), pl.ds(tokens, tokens))
    steps = n_z // 2
    up = [block] + list(blocks[: steps - 1])
    down = [block] + list(blocks[steps - 1 : 2 * steps - 2])
    opposite = blocks[2 * steps - 2]

    def hop(t, n, part):
        if t == steps - 1:
            return opposite.at[parts[part]] if part == n else None
        return (up, down)[n][t + 1].at[parts[part]]

    def ring(t, n, part):
        target = hop(t, n, part)
        if target is not None:
            source = (up, down)[n][t].at[parts[part]]
            to(
                source, target, ring_ss.at[n, t, part], ring_rs.at[n, t, part], my, (above, below)[n]
            ).start()

    def ring_wait(t, n, part):
        target = hop(t, n, part)
        if target is not None:
            wait_for(target, ring_rs.at[n, t, part])

    ways = [(n, part) for part in range(2) for n in range(2)]

    def share(rel, held):
        def one(d, carry):
            for side, s in enumerate((slot, other_slot)):
                first = (2 * d + s) * cap
                for c in range(cap):
                    token = table_smem[rel, 0, first + c]
                    sb[rel, side * plane + d, c] = held[token]
                    sb[rel, side * plane + d, cap + c] = held[
                        jnp.minimum(token + tokens, 2 * tokens)
                    ]
            return carry

        lax.fori_loop(0, plane, one, 0)

        def out(i, carry):
            d = lax.rem(inner + i, plane)
            for side, y in enumerate((my, partner)):
                to(
                    sb.at[rel, side * plane + d],
                    recv.at[rel, side * plane + inner],
                    tok_ss,
                    tok_rs.at[rel],
                    y,
                    z * plane + d,
                ).start()
            return carry

        to(
            sb.at[rel, plane + inner],
            recv.at[rel, plane + inner],
            tok_ss,
            tok_rs.at[rel],
            partner,
            me,
        ).start()
        lax.fori_loop(1, plane, out, 0)
        recv[rel, inner] = sb[rel, inner]

    for n, part in ways:
        ring(0, n, part)
    to(w.at[slot], wf.at[my], w_ss.at[0], w_rs.at[0], mate, me).start()
    to(w.at[other_slot], wf.at[my], w_ss.at[1], w_rs.at[1], partner, me).start()
    own_w = pltpu.make_async_copy(w.at[slot], wf.at[my], own_sem.at[0])
    own_w.start()
    for source, target, ss, rs in (
        (table, table_recv, table_ss, table_rs),
        (q_table, q_mid, qt_ss, qt_rs),
    ):
        for rel in range(1, n_z):
            to(
                source.at[lax.rem(z + rel, n_z)],
                target.at[n_z - rel],
                ss,
                rs,
                my,
                lax.rem(me + rel * plane, n_exp),
            ).start()
        target[0] = source[z]
    for held in blocks:
        held[2 * tokens] = jnp.zeros((slabs, LANES), BF16)
    back[2 * n_exp * cap] = jnp.zeros((slabs, LANES), BF16)
    wait_for(table_recv.at[pl.ds(0, n_z - 1)], table_rs)
    to_smem = pltpu.make_async_copy(table_recv, table_smem, own_sem.at[1])
    to_smem.start()
    wait_for(q_mid.at[pl.ds(0, n_z - 1)], qt_rs)

    def q_out(i, carry):
        e = z * plane + lax.rem(inner + i, plane)
        for side, y in enumerate((my, partner)):
            to(q_mid, q_all.at[side * plane + inner], q_ss, q_rs, y, e).start()
        return carry

    to(q_mid, q_all.at[plane + inner], q_ss, q_rs, partner, me).start()
    lax.fori_loop(1, plane, q_out, 0)
    q_all[inner] = q_mid[...]
    to_smem.wait()

    lanes = lax.broadcasted_iota(jnp.int32, (sides, LANES), 1)

    def to_matrix(rel, which, out):
        part = recv[rel, :, which * cap : (which + 1) * cap]
        flat[...] = part.astype(F32).reshape(group * slabs, LANES)

        def gather(p, carry):
            for b in range(per):
                for c in range(cap):
                    value = flat[pl.ds(c * slabs + p * per + b, sides, stride=cap * slabs), :]
                    first = rel * group + c * sides
                    out[p, first : first + sides, b * LANES : (b + 1) * LANES] = value.astype(BF16)
            return carry

        lax.fori_loop(0, n_dp, gather, 0)

    def process(rel):
        wait_for(recv.at[rel, pl.ds(0, sides - 1)], tok_rs.at[rel])
        here = slice(rel * group, (rel + 1) * group)
        to_matrix(rel, 0, xm)
        to_matrix(rel, 1, gm)
        weights = q_all[:, rel].reshape(sides, LANES)
        weight = jnp.concatenate(
            [
                jnp.sum(
                    jnp.where(lanes == (2 * inner + slot) * cap + c, weights, 0.0),
                    axis=1,
                    keepdims=True,
                )
                for c in range(cap)
            ],
            axis=0,
        )
        q_col[here] = jnp.broadcast_to(weight, (group, LANES))

        def project(p, carry):
            gate_up, down = carry
            gate_up = gate_up + jnp.dot(
                xm[p, here], wf[p, :, : 2 * ff], preferred_element_type=F32
            )
            down = down + jnp.dot(gm[p, here], wf[p, :, 2 * ff :], preferred_element_type=F32)
            return gate_up, down

        gate_up, down = lax.fori_loop(
            0, n_dp, project, (jnp.zeros((group, 2 * ff), F32), jnp.zeros((group, ff), F32))
        )
        gate, up_value = gate_up[:, :ff], gate_up[:, ff:]
        sig = jax.nn.sigmoid(gate)
        silu = gate * sig
        act = (silu * up_value).astype(BF16)
        act_s[here] = act
        grad = jnp.sum(act.astype(F32) * down, axis=1, keepdims=True).astype(BF16).astype(F32)
        act_grad = weight * down
        gu[here, :ff] = (act_grad * up_value * sig * (1.0 + gate * (1.0 - sig))).astype(BF16)
        gu[here, ff:] = (act_grad * silu).astype(BF16)
        grads = jnp.zeros((sides, LANES), F32)
        for c in range(cap):
            grads = jnp.where(
                lanes == (2 * inner + slot) * cap + c,
                grad[c * sides : (c + 1) * sides],
                grads,
            )
        pg[:, rel] = grads.reshape(sides, 1, LANES)

        def expand(p, carry):
            value = lax.dot_general(
                gu[here],
                wf[p, :, : 2 * ff],
                (((1,), (1,)), ((), ())),
                preferred_element_type=F32,
            )
            for b in range(per):
                for c in range(cap):
                    flat[pl.ds(c * slabs + p * per + b, sides, stride=cap * slabs), :] = value[
                        c * sides : (c + 1) * sides, b * LANES : (b + 1) * LANES
                    ]
            return carry

        lax.fori_loop(0, n_dp, expand, 0)
        dxs[rel] = flat[...].astype(BF16).reshape(sides, cap, slabs, LANES)

    def send_back(rel, source, target, ss, rs):
        first = lax.rem(z + rel, n_z) * plane

        def both(i, carry):
            d = lax.rem(inner + i, plane)
            for side, y in enumerate((my, partner)):
                to(source.at[rel, side * plane + d], target, ss, rs, y, first + d).start()
            return carry

        if rel:
            lax.fori_loop(0, plane, both, 0)
        else:
            to(source.at[rel, plane + inner], target, ss, rs, partner, me).start()
            lax.fori_loop(1, plane, both, 0)

    spot = slot * n_exp + me
    own_rows = pl.ds(spot * cap, cap)

    def pg_first():
        def both(i, carry):
            d = lax.rem(inner + i, plane)
            for side, y in enumerate((my, partner)):
                to(
                    pg.at[side * plane + d],
                    pg_in.at[side * plane + inner],
                    pg_ss,
                    pg_rs,
                    y,
                    z * plane + d,
                ).start()
            return carry

        to(
            pg.at[plane + inner], pg_in.at[plane + inner], pg_ss, pg_rs, partner, me
        ).start()
        lax.fori_loop(1, plane, both, 0)
        pg_in[inner] = pg[inner]

    def pg_second():
        wait_for(pg_in.at[pl.ds(0, sides - 1)], pg_rs)
        pg_mid[...] = jnp.sum(pg_in[...], axis=0)
        for rel in range(1, n_z):
            to(
                pg_mid.at[rel],
                pg_recv.at[n_z - rel],
                pm_ss,
                pm_rs,
                my,
                lax.rem(me + rel * plane, n_exp),
            ).start()
        pg_recv[0] = pg_mid[0]

    def dx_start(rel):
        send_back(rel, dxs, back.at[own_rows], dx_ss, dx_rs)
        if rel == 0:
            back[own_rows] = dxs[0, inner]

    def weight_grad(p):
        both = (((0,), (0,)), ((), ()))
        dwp[p, :, : 2 * ff] = lax.dot_general(
            xm[p], gu[...], both, preferred_element_type=F32
        ).astype(BF16)
        out_grad = jnp.concatenate(
            [
                (q_col[...] * gm[p, :, n * LANES : (n + 1) * LANES].astype(F32)).astype(BF16)
                for n in range(quarter // LANES)
            ],
            axis=1,
        )
        dwp[p, :, 2 * ff :] = lax.dot_general(
            out_grad, act_s[...], both, preferred_element_type=F32
        ).astype(BF16)

    share(0, block)
    waiting, done = [0], []
    for t in range(steps - 1):
        for n, part in ways:
            ring_wait(t, n, part)
            ring(t + 1, n, part)
        if t == 0:
            wait_for(wf.at[partner], w_rs.at[1])
            to(wf.at[partner], wf.at[partner], w_ss.at[2], w_rs.at[2], mate, me).start()
        share(n_z - t - 1, up[t + 1])
        share(t + 1, down[t + 1])
        if t == max(steps - 3, 0):
            own_w.wait()
            wait_for(wf.at[mate], w_rs.at[0])
            wait_for(wf.at[corner], w_rs.at[2])
            wait_for(q_all.at[pl.ds(0, sides - 1)], q_rs)
        if t >= steps - 3:
            for rel in waiting:
                process(rel)
            done += waiting
            waiting = []
        waiting += [n_z - t - 1, t + 1]
    for n, part in ways:
        ring_wait(steps - 1, n, part)
    share(steps, opposite)
    for rel in reversed(done[1:]):
        dx_start(rel)
    for rel in waiting:
        process(rel)
    process(steps)
    pg_first()

    def give(n, source, target, d):
        to(source, target, g_ss.at[n], g_rs.at[n], d, me).start()

    halves = [pl.ds(n * half, half) for n in range(2)]

    def relay(n):
        wait_for(from_mate.at[halves[n]], g_rs.at[n])
        dwp[partner, halves[n]] = (
            dwp[partner, halves[n]].astype(F32) + from_mate[halves[n]].astype(F32)
        ).astype(BF16)
        give(3 + n, dwp.at[partner, halves[n]], from_partner.at[halves[n]], partner)

    weight_grad(corner)
    for n in range(2):
        give(n, dwp.at[corner, halves[n]], from_mate.at[halves[n]], mate)
    for rel in waiting:
        dx_start(rel)
    dx_start(steps)
    weight_grad(mate)
    give(2, dwp.at[mate], from_mate2, mate)
    pg_second()
    weight_grad(partner)
    dx_start(0)
    relay(0)
    weight_grad(my)

    wait_for(pg_recv.at[pl.ds(0, n_z - 1)], pm_rs)
    grads = pg_recv[...].reshape(n_z, LANES).astype(BF16)
    fanout = te.shape[0]
    first_dims = (((0,), (0,)), ((), ()))
    planes = lax.rem(lax.broadcasted_iota(jnp.int32, (n_z, tokens), 0) + z, n_z)
    spots = lax.broadcasted_iota(jnp.int32, (LANES, tokens), 0)
    experts = lax.broadcasted_iota(jnp.int32, (n_exp, tokens), 0)
    pair = []
    weighted = jnp.zeros((1, tokens), F32)
    for k in range(fanout):
        hit = (plane_of[k : k + 1, :] == planes).astype(F32).astype(BF16)
        spread = lax.dot_general(grads, hit, first_dims, preferred_element_type=F32)
        value = jnp.sum(
            jnp.where(lane[k : k + 1, :] == spots, spread, 0.0), axis=0, keepdims=True
        )
        pair.append(value)
        weighted = weighted + probs[k : k + 1, :] * value
    logit = jnp.zeros((n_exp, tokens), F32)
    for k in range(fanout):
        chosen = probs[k : k + 1, :] * (pair[k] - weighted)
        logit = logit + jnp.where(te[k : k + 1, :] == experts, chosen, 0.0)
    logit = logit.astype(BF16)
    for a in range(slabs):
        flat[pl.ds(a, n_exp, stride=slabs), :] = jnp.dot(
            logit, x[:, a * LANES : (a + 1) * LANES], preferred_element_type=F32
        )
    rt[...] = flat[pl.ds(0, n_exp * slabs), :].astype(BF16).reshape(rt.shape)

    def rt_out(i, carry):
        d = lax.rem(me + i, n_exp)
        to(rt.at[d], rt_recv.at[me], rt_ss, rt_rs, my, d).start()
        return carry

    lax.fori_loop(1, n_exp, rt_out, 0)
    rt_recv[me] = rt[me]
    relay(1)
    wait_for(rt_recv.at[pl.ds(0, others)], rt_rs)
    r2[0] = jnp.sum(rt_recv[...].astype(F32), axis=0)
    for n, d in enumerate((mate, partner, corner)):
        to(r2.at[0], r2.at[n + 1], r2_ss.at[n], r2_rs.at[n], d, me).start()

    wait_for(back.at[pl.ds(0, (2 * n_exp - 1) * cap)], dx_rs)

    def combine(t, carry):
        total = back[place[t * fanout]].astype(F32)
        for k in range(1, fanout):
            total = total + back[place[t * fanout + k]].astype(F32)
        sums[pl.ds(pl.multiple_of(t * slabs, slabs), slabs), :] = total
        return carry

    lax.fori_loop(0, tokens, combine, 0)
    for a in range(slabs):
        cols = slice(a * LANES, (a + 1) * LANES)
        routed = lax.dot_general(logit, proj[:, cols], first_dims, preferred_element_type=F32)
        token_grad[:, cols] = (sums[pl.ds(a, tokens, stride=slabs), :] + routed).astype(BF16)

    for n in range(n_dp - 1):
        wait_for(r2.at[n + 1], r2_rs.at[n])
    sums[pl.ds(0, slabs), :] = r2[0] + r2[1] + r2[2] + r2[3]
    share_rows = slabs // n_dp
    rcol[...] = sums[pl.ds(my * share_rows, share_rows), :]
    outs = (gate_grad, up_grad, down_grad)
    for n in range(2):
        wait_for(from_partner.at[halves[n]], g_rs.at[3 + n])
    for n, out in enumerate(outs):
        cols = slice(n * ff, (n + 1) * ff)
        out[other_slot] = from_partner[:, cols].astype(F32)
    wait_for(from_mate2, g_rs.at[2])
    for n, out in enumerate(outs):
        cols = slice(n * ff, (n + 1) * ff)
        out[slot] = dwp[my, :, cols].astype(F32) + from_mate2[:, cols].astype(F32)

    for t in range(steps):
        for n, part in ways:
            if hop(t, n, part) is not None:
                wait_for(block.at[parts[part]], ring_ss.at[n, t, part])
    wait_for(table.at[pl.ds(0, n_z - 1)], table_ss)
    wait_for(q_table.at[pl.ds(0, n_z - 1)], qt_ss)
    wait_for(q_all.at[pl.ds(0, sides - 1)], q_ss)
    for rel in range(n_z):
        wait_for(recv.at[rel, pl.ds(0, sides - 1)], tok_ss)
    for n in range(3):
        wait_for(wf.at[0], w_ss.at[n])
    for n in (0, 1, 3, 4):
        wait_for(from_mate.at[pl.ds(0, half)], g_ss.at[n])
    wait_for(from_mate2, g_ss.at[2])
    wait_for(back.at[pl.ds(0, (2 * n_exp - 1) * cap)], dx_ss)
    wait_for(pg_in.at[pl.ds(0, sides - 1)], pg_ss)
    wait_for(pg_mid.at[pl.ds(0, n_z - 1)], pm_ss)
    wait_for(rt.at[pl.ds(0, others)], rt_ss)
    for n in range(n_dp - 1):
        wait_for(r2.at[0], r2_ss.at[n])


def exchange(n_dp, n_exp, place, table, q_table, w, x, g, proj, te, plane_of, lane, probs):
    slots, quarter, wide = w.shape
    cap = CAP
    slabs = x.shape[1] // LANES
    held = (2 * x.shape[0] + 1, slabs, LANES)
    n_z = table.shape[0]
    sides = 2 * n_exp // n_z
    group = sides * cap
    rows = n_z * group
    ff = wide // 3
    tokens, width = x.shape
    vmem = pl.BlockSpec(memory_space=pltpu.VMEM)
    hbm = pl.BlockSpec(memory_space=pl.ANY)
    smem = pl.BlockSpec(memory_space=pltpu.SMEM)
    dma = pltpu.SemaphoreType.DMA
    return pl.pallas_call(
        functools.partial(exchange_kernel, n_dp, n_exp),
        out_shape=(
            jax.ShapeDtypeStruct((tokens, width), BF16),
            jax.ShapeDtypeStruct((slots, quarter, ff), F32),
            jax.ShapeDtypeStruct((slots, quarter, ff), F32),
            jax.ShapeDtypeStruct((slots, quarter, ff), F32),
            jax.ShapeDtypeStruct((slabs // n_dp, LANES), F32),
        ),
        in_specs=[smem, vmem, vmem, hbm] + [vmem] * 7,
        out_specs=(vmem,) * 5,
        scratch_shapes=[
            pltpu.VMEM(held, BF16),
            pltpu.VMEM((n_z, sides, 2 * cap, slabs, LANES), BF16),
            pltpu.VMEM((n_z, sides, 2 * cap, slabs, LANES), BF16),
            pltpu.VMEM((n_z, sides, cap, slabs, LANES), BF16),
            pltpu.VMEM((2 * n_exp * cap + 1, slabs, LANES), BF16),
            pltpu.VMEM((n_z, 1, LANES), jnp.int32),
            pltpu.SMEM((n_z, 1, LANES), jnp.int32),
            pltpu.VMEM((n_z, 1, LANES), F32),
            pltpu.VMEM((sides, n_z, 1, LANES), F32),
            pltpu.VMEM((n_dp, quarter, wide), BF16),
            pltpu.VMEM((max(group, n_exp) * slabs, LANES), F32),
            pltpu.VMEM((n_dp, rows, quarter), BF16),
            pltpu.VMEM((n_dp, rows, quarter), BF16),
            pltpu.VMEM((rows, 2 * ff), BF16),
            pltpu.VMEM((rows, ff), BF16),
            pltpu.VMEM((rows, LANES), F32),
            pltpu.VMEM((n_dp, quarter, wide), BF16),
            pltpu.VMEM((quarter, wide), BF16),
            pltpu.VMEM((quarter, wide), BF16),
            pltpu.VMEM((quarter, wide), BF16),
            pltpu.VMEM((sides, n_z, 1, LANES), F32),
            pltpu.VMEM((sides, n_z, 1, LANES), F32),
            pltpu.VMEM((n_z, 1, LANES), F32),
            pltpu.VMEM((n_z, 1, LANES), F32),
            pltpu.VMEM((n_exp, slabs, LANES), BF16),
            pltpu.VMEM((n_exp, slabs, LANES), BF16),
            pltpu.VMEM((n_dp, slabs, LANES), F32),
            pltpu.VMEM((tokens * slabs, LANES), F32),
            dma((2, n_z // 2, 2)),
            dma((2, n_z // 2, 2)),
            dma,
            dma,
            dma,
            dma,
            dma,
            dma,
            dma,
            dma((n_z,)),
            dma((3,)),
            dma((3,)),
            dma((5,)),
            dma((5,)),
            dma,
            dma,
            dma,
            dma,
            dma,
            dma,
            dma,
            dma,
            dma((n_dp - 1,)),
            dma((n_dp - 1,)),
            dma((2,)),
        ]
        + [pltpu.VMEM(held, BF16)] * (n_z - 1),
        compiler_params=pltpu.CompilerParams(
            collective_id=0, has_side_effects=True, vmem_limit_bytes=60 * 1024 * 1024
        ),
    )(place, table, q_table, w, x, g, proj, te, plane_of, lane, probs)


def shards(
    n_dp,
    n_exp,
    layer_inputs,
    output_adjoint,
    dispatcher_projection,
    gating_kernel,
    expansion_kernel,
    contraction_kernel,
    token_experts,
    copy_choice_index,
    expert_copies,
    send_quotas,
):
    tokens, width = layer_inputs.shape
    fanout = token_experts.shape[1]
    experts = dispatcher_projection.shape[1]
    replicas = expert_copies.shape[1]
    position_count = send_quotas.shape[0]
    slots = gating_kernel.shape[1]
    hidden = gating_kernel.shape[2]
    slabs = width // LANES
    pairs = tokens * fanout
    sent = slots * n_exp * CAP

    logits = jnp.dot(layer_inputs, dispatcher_projection, preferred_element_type=F32)
    route_hit = token_experts[:, :, None] == lax.iota(jnp.int32, experts)[None, None, :]
    chosen = jnp.sum(jnp.where(route_hit, logits[:, None, :], 0.0), axis=2)
    probs = jax.nn.softmax(chosen, axis=1)
    flat_pick = (token_experts * replicas + copy_choice_index).reshape(pairs)
    target = jnp.sum(
        jnp.where(
            flat_pick[:, None] == lax.iota(jnp.int32, experts * replicas)[None, :],
            expert_copies.reshape(experts * replicas)[None, :],
            0,
        ),
        axis=1,
    )
    agrees = (target[:, None] == lax.iota(jnp.int32, position_count)[None, :]).astype(jnp.int32)
    arrival = jnp.sum((jnp.cumsum(agrees, axis=0) - agrees) * agrees, axis=1)
    bound = jnp.sum(agrees * send_quotas[None, :], axis=1)
    kept = arrival < bound
    owner = target // slots
    local = target % slots
    position = jnp.where(kept, (local * n_exp + owner) * CAP + arrival, sent)
    hit = position[None, :] == lax.iota(jnp.int32, sent)[:, None]
    pair_token = lax.iota(jnp.int32, pairs) // fanout
    pick = 2 * tokens - jnp.sum(jnp.where(hit, 2 * tokens - pair_token[None, :], 0), axis=1)
    sent_prob = probs.astype(BF16).astype(F32).reshape(1, pairs)
    prob = jnp.sum(jnp.where(hit, sent_prob, 0.0), axis=1)
    n_z = n_exp // PLANE

    def by_plane(values):
        count = slots * PLANE * CAP
        values = values.reshape(slots, n_z, PLANE, CAP).transpose(1, 2, 0, 3)
        return jnp.pad(values.reshape(n_z, 1, count), ((0, 0), (0, 0), (0, LANES - count)))

    table, q_table = by_plane(pick), by_plane(prob)
    weights = jnp.concatenate(
        [gating_kernel, expansion_kernel, contraction_kernel], axis=2
    ).transpose(1, 0, 2)
    plane_of = jnp.where(kept, owner // PLANE, -1).reshape(tokens, fanout).T
    lane = (((owner % PLANE) * slots + local) * CAP + arrival).reshape(tokens, fanout).T
    token_grad, gate_grad, up_grad, down_grad, router = exchange(
        n_dp,
        n_exp,
        position,
        table,
        q_table,
        weights,
        layer_inputs,
        output_adjoint,
        dispatcher_projection.T,
        token_experts.T,
        plane_of,
        lane,
        probs.T,
    )
    gate_grad, up_grad, down_grad = (
        grad.transpose(1, 0, 2) for grad in (gate_grad, up_grad, down_grad)
    )
    router_grad = router.reshape(width // n_dp, 1)
    return (token_grad, gate_grad, up_grad, down_grad, router_grad)


def solution(mesh):
    return jax.shard_map(
        functools.partial(shards, mesh.shape["dp"], mesh.shape["expert"]),
        mesh=mesh,
        in_specs=(
            P(("dp", "expert"), None),
            P(("dp", "expert"), None),
            P(),
            P("dp", "expert", None),
            P("dp", "expert", None),
            P("dp", "expert", None),
            P(("dp", "expert"), None),
            P(("dp", "expert"), None),
            P(),
            P(),
        ),
        out_specs=(
            P(("dp", "expert"), None),
            P("dp", "expert", None),
            P("dp", "expert", None),
            P("dp", "expert", None),
            P("dp", "expert"),
        ),
        check_vma=False,
    )
```

```python
import functools

import jax
import jax.numpy as jnp
from jax import lax
from jax.experimental import pallas as pl
from jax.experimental.pallas import tpu as pltpu
from jax.sharding import PartitionSpec as P

CAP = 5
PLANE = 8
LANES = 128
MESH = pl.DeviceIdType.MESH
F32 = jnp.float32
BF16 = jnp.bfloat16


def exchange_kernel(
    n_dp,
    n_exp,
    w,
    x,
    g,
    proj,
    te,
    choice,
    copies,
    quotas,
    token_grad,
    gate_grad,
    up_grad,
    down_grad,
    rcol,
    table,
    q_table,
    plane_of,
    lane,
    probs,
    spots_of,
    place,
    block,
    recv,
    sb,
    dxs,
    back,
    table_recv,
    table_smem,
    q_mid,
    q_all,
    wf,
    flat,
    xm,
    gm,
    gu,
    act_s,
    q_col,
    dwp,
    from_mate,
    from_mate2,
    from_partner,
    pg,
    pg_in,
    pg_mid,
    pg_recv,
    rt,
    rt_recv,
    r2,
    sums,
    ring_ss,
    ring_rs,
    table_ss,
    table_rs,
    qt_ss,
    qt_rs,
    q_ss,
    q_rs,
    tok_ss,
    tok_rs,
    w_ss,
    w_rs,
    g_ss,
    g_rs,
    dx_ss,
    dx_rs,
    pg_ss,
    pg_rs,
    pm_ss,
    pm_rs,
    rt_ss,
    rt_rs,
    r2_ss,
    r2_rs,
    own_sem,
    *blocks,
):
    me = lax.axis_index("expert")
    my = lax.axis_index("dp")
    partner = n_dp - 1 - my
    slot = lax.div(my, 2)
    other_slot = 1 - slot
    mate = my + 1 - 2 * lax.rem(my, 2)
    corner = n_dp - 1 - mate
    n_z, sides, depth, slabs, _ = sb.shape
    plane = sides // 2
    cap = depth // 2
    group = sides * cap
    rows = n_z * group
    tokens = x.shape[0]
    z, inner = lax.div(me, plane), lax.rem(me, plane)
    above, below = lax.rem(me + plane, n_exp), lax.rem(me + n_exp - plane, n_exp)
    quarter = wf.shape[1]
    half = quarter // 2
    ff = wf.shape[2] // 3
    per = slabs // n_dp
    others = n_exp - 1

    barrier = pltpu.get_barrier_semaphore()

    def greet(d, e):
        pl.semaphore_signal(
            barrier, inc=1, device_id={"dp": d, "expert": e}, device_id_type=MESH
        )

    def greet_both(i, carry):
        greet(my, lax.rem(me + i, n_exp))
        greet(partner, lax.rem(me + i, n_exp))
        return carry

    greet(mate, me)
    greet(corner, me)
    greet(partner, me)
    lax.fori_loop(1, n_exp, greet_both, 0)
    for which, ref in enumerate((x, g)):
        for a in range(slabs):
            sums[pl.ds(a, tokens, stride=slabs), :] = ref[:, a * LANES : (a + 1) * LANES].astype(F32)
        block[which * tokens : (which + 1) * tokens] = (
            sums[...].astype(BF16).reshape(tokens, slabs, LANES)
        )
    block[2 * tokens] = jnp.zeros((slabs, LANES), BF16)
    pl.semaphore_wait(barrier, 2 * n_exp + 1)

    def to(src, dst, ss, rs, d, e):
        return pltpu.make_async_remote_copy(
            src, dst, ss, rs, device_id={"dp": d, "expert": e}, device_id_type=MESH
        )

    def wait_for(ref, sem):
        pltpu.make_async_copy(ref, ref, sem).wait()

    parts = (pl.ds(0, tokens), pl.ds(tokens, tokens))
    steps = n_z // 2
    up = [block] + list(blocks[: steps - 1])
    down = [block] + list(blocks[steps - 1 : 2 * steps - 2])
    opposite = blocks[2 * steps - 2]

    def hop(t, n, part):
        if t == steps - 1:
            return opposite.at[parts[part]] if part == n else None
        return (up, down)[n][t + 1].at[parts[part]]

    def ring(t, n, part):
        target = hop(t, n, part)
        if target is not None:
            source = (up, down)[n][t].at[parts[part]]
            to(
                source, target, ring_ss.at[n, t, part], ring_rs.at[n, t, part], my, (above, below)[n]
            ).start()

    def ring_wait(t, n, part):
        target = hop(t, n, part)
        if target is not None:
            wait_for(target, ring_rs.at[n, t, part])

    ways = [(n, part) for part in range(2) for n in range(2)]

    def share(rel, held):
        def one(d, carry):
            for side, s in enumerate((slot, other_slot)):
                first = (2 * d + s) * cap
                for c in range(cap):
                    token = jnp.clip(table_smem[rel, 0, first + c], 0, 2 * tokens)
                    sb[rel, side * plane + d, c] = held[token]
                    sb[rel, side * plane + d, cap + c] = held[
                        jnp.minimum(token + tokens, 2 * tokens)
                    ]
            return carry

        lax.fori_loop(0, plane, one, 0)

        def out(i, carry):
            d = lax.rem(inner + i, plane)
            for side, y in enumerate((my, partner)):
                to(
                    sb.at[rel, side * plane + d],
                    recv.at[rel, side * plane + inner],
                    tok_ss,
                    tok_rs.at[rel],
                    y,
                    z * plane + d,
                ).start()
            return carry

        to(
            sb.at[rel, plane + inner],
            recv.at[rel, plane + inner],
            tok_ss,
            tok_rs.at[rel],
            partner,
            me,
        ).start()
        lax.fori_loop(1, plane, out, 0)
        recv[rel, inner] = sb[rel, inner]

    fanout = te.shape[0]
    last_dims = (((1,), (1,)), ((), ()))

    def route():
        ids = lambda count: lax.broadcasted_iota(jnp.int32, (count, tokens), 0)
        flag = lambda hit: hit.astype(F32).astype(BF16)
        matmul = lambda a, b: jnp.dot(a, b, preferred_element_type=F32)
        experts, replicas = proj.shape[0], copies.shape[1] // proj.shape[0]
        logits = lax.dot_general(proj[...], x[...], last_dims, preferred_element_type=F32)
        chosen = jnp.concatenate(
            [
                jnp.sum(
                    jnp.where(te[k : k + 1, :] == ids(experts), logits, 0.0), axis=0, keepdims=True
                )
                for k in range(fanout)
            ],
            axis=0,
        )
        powers = jnp.exp(chosen - jnp.max(chosen, axis=0, keepdims=True))
        probs[...] = powers / jnp.sum(powers, axis=0, keepdims=True)
        slot_row = jnp.broadcast_to(copies[...].astype(F32), (16, copies.shape[1])).astype(BF16)
        quota_row = jnp.broadcast_to(quotas[...].astype(F32), (16, quotas.shape[1])).astype(BF16)
        targets, hits = [], []
        for k in range(fanout):
            pick = te[k : k + 1, :] * replicas + choice[k : k + 1, :]
            target = matmul(slot_row, flag(pick == ids(copies.shape[1])))[0:1].astype(jnp.int32)
            targets.append(target)
            hits.append(target == ids(quotas.shape[1]))
        count = sum(hit.astype(F32) for hit in hits).astype(BF16)
        earlier = lax.broadcasted_iota(jnp.int32, (tokens, tokens), 0) < lax.broadcasted_iota(
            jnp.int32, (tokens, tokens), 1
        )
        ahead = matmul(count, flag(earlier))
        value = 2 * tokens - lax.broadcasted_iota(jnp.int32, (n_z, tokens), 1)
        picks = jnp.zeros((n_z, LANES), F32)
        weights = jnp.zeros((n_z, LANES), F32)
        n_slots = w.shape[0]
        for k in range(fanout):
            arrival = jnp.sum(jnp.where(hits[k], ahead, 0.0), axis=0, keepdims=True)
            kept = arrival < matmul(quota_row, flag(hits[k]))[0:1]
            arrival = arrival.astype(jnp.int32)
            owner, local = lax.div(targets[k], n_slots), lax.rem(targets[k], n_slots)
            to_plane = jnp.where(kept, lax.div(owner, plane), -1)
            spot_lane = (lax.rem(owner, plane) * n_slots + local) * cap + arrival
            plane_of[k : k + 1, :] = to_plane
            lane[k : k + 1, :] = spot_lane
            spots_of[k : k + 1, :] = jnp.where(
                kept, (local * n_exp + owner) * cap + arrival, n_slots * n_exp * cap
            )
            there = to_plane == ids(n_z)
            spread = flag(spot_lane == ids(LANES))
            picks = picks + lax.dot_general(
                jnp.where(there, value, 0).astype(F32).astype(BF16),
                spread,
                last_dims,
                preferred_element_type=F32,
            )
            weights = weights + lax.dot_general(
                jnp.where(there, probs[k : k + 1, :], 0.0).astype(BF16),
                spread,
                last_dims,
                preferred_element_type=F32,
            )
        picks = jnp.clip(picks, 0.0, 2.0 * tokens).astype(jnp.int32)
        table[...] = jnp.clip(2 * tokens - picks, 0, 2 * tokens).reshape(table.shape)
        q_table[...] = weights.reshape(q_table.shape)

    for n, part in ways:
        ring(0, n, part)
    to(w.at[slot], wf.at[my], w_ss.at[0], w_rs.at[0], mate, me).start()
    to(w.at[other_slot], wf.at[my], w_ss.at[1], w_rs.at[1], partner, me).start()
    own_w = pltpu.make_async_copy(w.at[slot], wf.at[my], own_sem.at[0])
    own_w.start()
    route()
    to_place = pltpu.make_async_copy(spots_of, place, own_sem.at[2])
    to_place.start()
    for source, target, ss, rs in (
        (table, table_recv, table_ss, table_rs),
        (q_table, q_mid, qt_ss, qt_rs),
    ):
        for rel in range(1, n_z):
            to(
                source.at[lax.rem(z + rel, n_z)],
                target.at[n_z - rel],
                ss,
                rs,
                my,
                lax.rem(me + rel * plane, n_exp),
            ).start()
        target[0] = source[z]
    for held in blocks:
        held[2 * tokens] = jnp.zeros((slabs, LANES), BF16)
    back[2 * n_exp * cap] = jnp.zeros((slabs, LANES), BF16)
    wait_for(table_recv.at[pl.ds(0, n_z - 1)], table_rs)
    to_smem = pltpu.make_async_copy(table_recv, table_smem, own_sem.at[1])
    to_smem.start()
    wait_for(q_mid.at[pl.ds(0, n_z - 1)], qt_rs)

    def q_out(i, carry):
        e = z * plane + lax.rem(inner + i, plane)
        for side, y in enumerate((my, partner)):
            to(q_mid, q_all.at[side * plane + inner], q_ss, q_rs, y, e).start()
        return carry

    to(q_mid, q_all.at[plane + inner], q_ss, q_rs, partner, me).start()
    lax.fori_loop(1, plane, q_out, 0)
    q_all[inner] = q_mid[...]
    to_smem.wait()

    lanes = lax.broadcasted_iota(jnp.int32, (sides, LANES), 1)

    def to_matrix(rel, which, out):
        part = recv[rel, :, which * cap : (which + 1) * cap]
        flat[...] = part.astype(F32).reshape(group * slabs, LANES)

        def gather(p, carry):
            for b in range(per):
                for c in range(cap):
                    value = flat[pl.ds(c * slabs + p * per + b, sides, stride=cap * slabs), :]
                    first = rel * group + c * sides
                    out[p, first : first + sides, b * LANES : (b + 1) * LANES] = value.astype(BF16)
            return carry

        lax.fori_loop(0, n_dp, gather, 0)

    def process(rel):
        wait_for(recv.at[rel, pl.ds(0, sides - 1)], tok_rs.at[rel])
        here = slice(rel * group, (rel + 1) * group)
        to_matrix(rel, 0, xm)
        to_matrix(rel, 1, gm)
        weights = q_all[:, rel].reshape(sides, LANES)
        weight = jnp.concatenate(
            [
                jnp.sum(
                    jnp.where(lanes == (2 * inner + slot) * cap + c, weights, 0.0),
                    axis=1,
                    keepdims=True,
                )
                for c in range(cap)
            ],
            axis=0,
        )
        q_col[here] = jnp.broadcast_to(weight, (group, LANES))

        def project(p, carry):
            gate_up, down = carry
            gate_up = gate_up + jnp.dot(
                xm[p, here], wf[p, :, : 2 * ff], preferred_element_type=F32
            )
            down = down + jnp.dot(gm[p, here], wf[p, :, 2 * ff :], preferred_element_type=F32)
            return gate_up, down

        gate_up, down = lax.fori_loop(
            0, n_dp, project, (jnp.zeros((group, 2 * ff), F32), jnp.zeros((group, ff), F32))
        )
        gate, up_value = gate_up[:, :ff], gate_up[:, ff:]
        sig = jax.nn.sigmoid(gate)
        silu = gate * sig
        act = (silu * up_value).astype(BF16)
        act_s[here] = act
        grad = jnp.sum(act.astype(F32) * down, axis=1, keepdims=True).astype(BF16).astype(F32)
        act_grad = weight * down
        gu[here, :ff] = (act_grad * up_value * sig * (1.0 + gate * (1.0 - sig))).astype(BF16)
        gu[here, ff:] = (act_grad * silu).astype(BF16)
        grads = jnp.zeros((sides, LANES), F32)
        for c in range(cap):
            grads = jnp.where(
                lanes == (2 * inner + slot) * cap + c,
                grad[c * sides : (c + 1) * sides],
                grads,
            )
        pg[:, rel] = grads.reshape(sides, 1, LANES)

        def expand(p, carry):
            value = lax.dot_general(
                gu[here],
                wf[p, :, : 2 * ff],
                (((1,), (1,)), ((), ())),
                preferred_element_type=F32,
            )
            for b in range(per):
                for c in range(cap):
                    flat[pl.ds(c * slabs + p * per + b, sides, stride=cap * slabs), :] = value[
                        c * sides : (c + 1) * sides, b * LANES : (b + 1) * LANES
                    ]
            return carry

        lax.fori_loop(0, n_dp, expand, 0)
        dxs[rel] = flat[...].astype(BF16).reshape(sides, cap, slabs, LANES)

    def send_back(rel, source, target, ss, rs):
        first = lax.rem(z + rel, n_z) * plane

        def both(i, carry):
            d = lax.rem(inner + i, plane)
            for side, y in enumerate((my, partner)):
                to(source.at[rel, side * plane + d], target, ss, rs, y, first + d).start()
            return carry

        if rel:
            lax.fori_loop(0, plane, both, 0)
        else:
            to(source.at[rel, plane + inner], target, ss, rs, partner, me).start()
            lax.fori_loop(1, plane, both, 0)

    spot = slot * n_exp + me
    own_rows = pl.ds(spot * cap, cap)

    def dx_start(rel):
        send_back(rel, dxs, back.at[own_rows], dx_ss, dx_rs)
        if rel == 0:
            back[own_rows] = dxs[0, inner]

    def pg_first():
        def both(i, carry):
            d = lax.rem(inner + i, plane)
            for side, y in enumerate((my, partner)):
                to(
                    pg.at[side * plane + d],
                    pg_in.at[side * plane + inner],
                    pg_ss,
                    pg_rs,
                    y,
                    z * plane + d,
                ).start()
            return carry

        to(
            pg.at[plane + inner], pg_in.at[plane + inner], pg_ss, pg_rs, partner, me
        ).start()
        lax.fori_loop(1, plane, both, 0)
        pg_in[inner] = pg[inner]

    def pg_second():
        wait_for(pg_in.at[pl.ds(0, sides - 1)], pg_rs)
        pg_mid[...] = jnp.sum(pg_in[...], axis=0)
        for rel in range(1, n_z):
            to(
                pg_mid.at[rel],
                pg_recv.at[n_z - rel],
                pm_ss,
                pm_rs,
                my,
                lax.rem(me + rel * plane, n_exp),
            ).start()
        pg_recv[0] = pg_mid[0]

    def weight_grad(p):
        both = (((0,), (0,)), ((), ()))
        dwp[p, :, : 2 * ff] = lax.dot_general(
            xm[p], gu[...], both, preferred_element_type=F32
        ).astype(BF16)
        out_grad = jnp.concatenate(
            [
                (q_col[...] * gm[p, :, n * LANES : (n + 1) * LANES].astype(F32)).astype(BF16)
                for n in range(quarter // LANES)
            ],
            axis=1,
        )
        dwp[p, :, 2 * ff :] = lax.dot_general(
            out_grad, act_s[...], both, preferred_element_type=F32
        ).astype(BF16)

    share(0, block)
    waiting, done = [0], []
    for t in range(steps - 1):
        for n, part in ways:
            ring_wait(t, n, part)
            ring(t + 1, n, part)
        if t == 0:
            wait_for(wf.at[partner], w_rs.at[1])
            to(wf.at[partner], wf.at[partner], w_ss.at[2], w_rs.at[2], mate, me).start()
        share(n_z - t - 1, up[t + 1])
        share(t + 1, down[t + 1])
        if t == max(steps - 3, 0):
            own_w.wait()
            wait_for(wf.at[mate], w_rs.at[0])
            wait_for(wf.at[corner], w_rs.at[2])
            wait_for(q_all.at[pl.ds(0, sides - 1)], q_rs)
        if t >= steps - 3:
            for rel in waiting:
                process(rel)
            done += waiting
            waiting = []
        waiting += [n_z - t - 1, t + 1]
    for n, part in ways:
        ring_wait(steps - 1, n, part)
    share(steps, opposite)
    for rel in reversed(done[1:]):
        dx_start(rel)
    for rel in waiting:
        process(rel)
    process(steps)
    pg_first()

    def give(n, source, target, d):
        to(source, target, g_ss.at[n], g_rs.at[n], d, me).start()

    halves = [pl.ds(n * half, half) for n in range(2)]

    def relay(n):
        wait_for(from_mate.at[halves[n]], g_rs.at[n])
        dwp[partner, halves[n]] = (
            dwp[partner, halves[n]].astype(F32) + from_mate[halves[n]].astype(F32)
        ).astype(BF16)
        give(3 + n, dwp.at[partner, halves[n]], from_partner.at[halves[n]], partner)

    weight_grad(corner)
    for n in range(2):
        give(n, dwp.at[corner, halves[n]], from_mate.at[halves[n]], mate)
    for rel in waiting:
        dx_start(rel)
    dx_start(steps)
    weight_grad(mate)
    give(2, dwp.at[mate], from_mate2, mate)
    pg_second()
    weight_grad(partner)
    dx_start(0)
    relay(0)
    weight_grad(my)

    wait_for(pg_recv.at[pl.ds(0, n_z - 1)], pm_rs)
    grads = pg_recv[...].reshape(n_z, LANES).astype(BF16)
    first_dims = (((0,), (0,)), ((), ()))
    planes = lax.rem(lax.broadcasted_iota(jnp.int32, (n_z, tokens), 0) + z, n_z)
    spots = lax.broadcasted_iota(jnp.int32, (LANES, tokens), 0)
    experts = lax.broadcasted_iota(jnp.int32, (n_exp, tokens), 0)
    pair = []
    weighted = jnp.zeros((1, tokens), F32)
    for k in range(fanout):
        hit = (plane_of[k : k + 1, :] == planes).astype(F32).astype(BF16)
        spread = lax.dot_general(grads, hit, first_dims, preferred_element_type=F32)
        value = jnp.sum(
            jnp.where(lane[k : k + 1, :] == spots, spread, 0.0), axis=0, keepdims=True
        )
        pair.append(value)
        weighted = weighted + probs[k : k + 1, :] * value
    logit = jnp.zeros((n_exp, tokens), F32)
    for k in range(fanout):
        chosen = probs[k : k + 1, :] * (pair[k] - weighted)
        logit = logit + jnp.where(te[k : k + 1, :] == experts, chosen, 0.0)
    logit = logit.astype(BF16)
    for a in range(slabs):
        flat[pl.ds(a, n_exp, stride=slabs), :] = jnp.dot(
            logit, x[:, a * LANES : (a + 1) * LANES], preferred_element_type=F32
        )
    rt[...] = flat[pl.ds(0, n_exp * slabs), :].astype(BF16).reshape(rt.shape)

    def rt_out(i, carry):
        d = lax.rem(me + i, n_exp)
        to(rt.at[d], rt_recv.at[me], rt_ss, rt_rs, my, d).start()
        return carry

    lax.fori_loop(1, n_exp, rt_out, 0)
    rt_recv[me] = rt[me]
    relay(1)
    wait_for(rt_recv.at[pl.ds(0, others)], rt_rs)
    r2[0] = jnp.sum(rt_recv[...].astype(F32), axis=0)
    for n, d in enumerate((mate, partner, corner)):
        to(r2.at[0], r2.at[n + 1], r2_ss.at[n], r2_rs.at[n], d, me).start()

    wait_for(back.at[pl.ds(0, (2 * n_exp - 1) * cap)], dx_rs)

    to_place.wait()

    def combine(t, carry):
        def row(k):
            return back[jnp.clip(place[k, t], 0, 2 * n_exp * cap)].astype(F32)

        total = row(0)
        for k in range(1, fanout):
            total = total + row(k)
        sums[pl.ds(pl.multiple_of(t * slabs, slabs), slabs), :] = total
        return carry

    lax.fori_loop(0, tokens, combine, 0)
    for a in range(slabs):
        cols = slice(a * LANES, (a + 1) * LANES)
        routed = lax.dot_general(logit, proj[:, cols], first_dims, preferred_element_type=F32)
        token_grad[:, cols] = (sums[pl.ds(a, tokens, stride=slabs), :] + routed).astype(BF16)

    for n in range(n_dp - 1):
        wait_for(r2.at[n + 1], r2_rs.at[n])
    sums[pl.ds(0, slabs), :] = r2[0] + r2[1] + r2[2] + r2[3]
    share_rows = slabs // n_dp
    rcol[...] = sums[pl.ds(my * share_rows, share_rows), :]
    outs = (gate_grad, up_grad, down_grad)
    for n in range(2):
        wait_for(from_partner.at[halves[n]], g_rs.at[3 + n])
    for n, out in enumerate(outs):
        cols = slice(n * ff, (n + 1) * ff)
        out[other_slot] = from_partner[:, cols].astype(F32)
    wait_for(from_mate2, g_rs.at[2])
    for n, out in enumerate(outs):
        cols = slice(n * ff, (n + 1) * ff)
        out[slot] = dwp[my, :, cols].astype(F32) + from_mate2[:, cols].astype(F32)

    for t in range(steps):
        for n, part in ways:
            if hop(t, n, part) is not None:
                wait_for(block.at[parts[part]], ring_ss.at[n, t, part])
    wait_for(table.at[pl.ds(0, n_z - 1)], table_ss)
    wait_for(q_table.at[pl.ds(0, n_z - 1)], qt_ss)
    wait_for(q_all.at[pl.ds(0, sides - 1)], q_ss)
    for rel in range(n_z):
        wait_for(recv.at[rel, pl.ds(0, sides - 1)], tok_ss)
    for n in range(3):
        wait_for(wf.at[0], w_ss.at[n])
    for n in (0, 1, 3, 4):
        wait_for(from_mate.at[pl.ds(0, half)], g_ss.at[n])
    wait_for(from_mate2, g_ss.at[2])
    wait_for(back.at[pl.ds(0, (2 * n_exp - 1) * cap)], dx_ss)
    wait_for(pg_in.at[pl.ds(0, sides - 1)], pg_ss)
    wait_for(pg_mid.at[pl.ds(0, n_z - 1)], pm_ss)
    wait_for(rt.at[pl.ds(0, others)], rt_ss)
    for n in range(n_dp - 1):
        wait_for(r2.at[0], r2_ss.at[n])


def exchange(n_dp, n_exp, w, x, g, proj, te, choice, copies, quotas):
    slots, quarter, wide = w.shape
    cap = CAP
    slabs = x.shape[1] // LANES
    held = (2 * x.shape[0] + 1, slabs, LANES)
    n_z = n_exp // PLANE
    fanout = te.shape[0]
    sides = 2 * n_exp // n_z
    group = sides * cap
    rows = n_z * group
    ff = wide // 3
    tokens, width = x.shape
    vmem = pl.BlockSpec(memory_space=pltpu.VMEM)
    hbm = pl.BlockSpec(memory_space=pl.ANY)
    dma = pltpu.SemaphoreType.DMA
    return pl.pallas_call(
        functools.partial(exchange_kernel, n_dp, n_exp),
        out_shape=(
            jax.ShapeDtypeStruct((tokens, width), BF16),
            jax.ShapeDtypeStruct((slots, quarter, ff), F32),
            jax.ShapeDtypeStruct((slots, quarter, ff), F32),
            jax.ShapeDtypeStruct((slots, quarter, ff), F32),
            jax.ShapeDtypeStruct((slabs // n_dp, LANES), F32),
        ),
        in_specs=[hbm] + [vmem] * 7,
        out_specs=(vmem,) * 5,
        scratch_shapes=[
            pltpu.VMEM((n_z, 1, LANES), jnp.int32),
            pltpu.VMEM((n_z, 1, LANES), F32),
            pltpu.VMEM((fanout, tokens), jnp.int32),
            pltpu.VMEM((fanout, tokens), jnp.int32),
            pltpu.VMEM((fanout, tokens), F32),
            pltpu.VMEM((fanout, tokens), jnp.int32),
            pltpu.SMEM((fanout, tokens), jnp.int32),
            pltpu.VMEM(held, BF16),
            pltpu.VMEM((n_z, sides, 2 * cap, slabs, LANES), BF16),
            pltpu.VMEM((n_z, sides, 2 * cap, slabs, LANES), BF16),
            pltpu.VMEM((n_z, sides, cap, slabs, LANES), BF16),
            pltpu.VMEM((2 * n_exp * cap + 1, slabs, LANES), BF16),
            pltpu.VMEM((n_z, 1, LANES), jnp.int32),
            pltpu.SMEM((n_z, 1, LANES), jnp.int32),
            pltpu.VMEM((n_z, 1, LANES), F32),
            pltpu.VMEM((sides, n_z, 1, LANES), F32),
            pltpu.VMEM((n_dp, quarter, wide), BF16),
            pltpu.VMEM((max(group, n_exp) * slabs, LANES), F32),
            pltpu.VMEM((n_dp, rows, quarter), BF16),
            pltpu.VMEM((n_dp, rows, quarter), BF16),
            pltpu.VMEM((rows, 2 * ff), BF16),
            pltpu.VMEM((rows, ff), BF16),
            pltpu.VMEM((rows, LANES), F32),
            pltpu.VMEM((n_dp, quarter, wide), BF16),
            pltpu.VMEM((quarter, wide), BF16),
            pltpu.VMEM((quarter, wide), BF16),
            pltpu.VMEM((quarter, wide), BF16),
            pltpu.VMEM((sides, n_z, 1, LANES), F32),
            pltpu.VMEM((sides, n_z, 1, LANES), F32),
            pltpu.VMEM((n_z, 1, LANES), F32),
            pltpu.VMEM((n_z, 1, LANES), F32),
            pltpu.VMEM((n_exp, slabs, LANES), BF16),
            pltpu.VMEM((n_exp, slabs, LANES), BF16),
            pltpu.VMEM((n_dp, slabs, LANES), F32),
            pltpu.VMEM((tokens * slabs, LANES), F32),
            dma((2, n_z // 2, 2)),
            dma((2, n_z // 2, 2)),
            dma,
            dma,
            dma,
            dma,
            dma,
            dma,
            dma,
            dma((n_z,)),
            dma((3,)),
            dma((3,)),
            dma((5,)),
            dma((5,)),
            dma,
            dma,
            dma,
            dma,
            dma,
            dma,
            dma,
            dma,
            dma((n_dp - 1,)),
            dma((n_dp - 1,)),
            dma((3,)),
        ]
        + [pltpu.VMEM(held, BF16)] * (n_z - 1),
        compiler_params=pltpu.CompilerParams(
            collective_id=0, has_side_effects=True, vmem_limit_bytes=60 * 1024 * 1024
        ),
    )(w, x, g, proj, te, choice, copies, quotas)


def shards(
    n_dp,
    n_exp,
    layer_inputs,
    output_adjoint,
    dispatcher_projection,
    gating_kernel,
    expansion_kernel,
    contraction_kernel,
    token_experts,
    copy_choice_index,
    expert_copies,
    send_quotas,
):
    width = layer_inputs.shape[1]

    weights = jnp.concatenate(
        [gating_kernel, expansion_kernel, contraction_kernel], axis=2
    ).transpose(1, 0, 2)
    token_grad, gate_grad, up_grad, down_grad, router = exchange(
        n_dp,
        n_exp,
        weights,
        layer_inputs,
        output_adjoint,
        dispatcher_projection.T,
        token_experts.T,
        copy_choice_index.T,
        expert_copies.reshape(1, -1),
        send_quotas.reshape(1, -1),
    )
    gate_grad, up_grad, down_grad = (
        grad.transpose(1, 0, 2) for grad in (gate_grad, up_grad, down_grad)
    )
    router_grad = router.reshape(width // n_dp, 1)
    return (token_grad, gate_grad, up_grad, down_grad, router_grad)


def solution(mesh):
    return jax.shard_map(
        functools.partial(shards, mesh.shape["dp"], mesh.shape["expert"]),
        mesh=mesh,
        in_specs=(
            P(("dp", "expert"), None),
            P(("dp", "expert"), None),
            P(),
            P("dp", "expert", None),
            P("dp", "expert", None),
            P("dp", "expert", None),
            P(("dp", "expert"), None),
            P(("dp", "expert"), None),
            P(),
            P(),
        ),
        out_specs=(
            P(("dp", "expert"), None),
            P("dp", "expert", None),
            P("dp", "expert", None),
            P("dp", "expert", None),
            P("dp", "expert"),
        ),
        check_vma=False,
    )
```

```python
import functools

import jax
import jax.numpy as jnp
from jax import lax
from jax.experimental import pallas as pl
from jax.experimental.pallas import tpu as pltpu
from jax.sharding import PartitionSpec as P

CAP = 5
PLANE = 8
LANES = 128
MESH = pl.DeviceIdType.MESH
F32 = jnp.float32
BF16 = jnp.bfloat16


def exchange_kernel(
    n_dp,
    n_exp,
    w,
    x,
    g,
    proj,
    te,
    choice,
    copies,
    quotas,
    token_grad,
    gate_grad,
    up_grad,
    down_grad,
    rcol,
    table,
    q_table,
    plane_of,
    lane,
    probs,
    spots_of,
    place,
    block,
    recv,
    sb,
    dxs,
    back,
    table_recv,
    table_smem,
    q_mid,
    q_all,
    wf,
    flat,
    xm,
    gm,
    gu,
    act_s,
    q_col,
    dwp,
    from_mate,
    from_mate2,
    from_partner,
    pg,
    pg_in,
    pg_mid,
    pg_recv,
    rt,
    rt_recv,
    r2,
    sums,
    ring_ss,
    ring_rs,
    table_ss,
    table_rs,
    qt_ss,
    qt_rs,
    q_ss,
    q_rs,
    tok_ss,
    tok_rs,
    w_ss,
    w_rs,
    g_ss,
    g_rs,
    dx_ss,
    dx_rs,
    pg_ss,
    pg_rs,
    pm_ss,
    pm_rs,
    rt_ss,
    rt_rs,
    r2_ss,
    r2_rs,
    own_sem,
    *blocks,
):
    me = lax.axis_index("expert")
    my = lax.axis_index("dp")
    partner = n_dp - 1 - my
    slot = lax.div(my, 2)
    other_slot = 1 - slot
    mate = my + 1 - 2 * lax.rem(my, 2)
    corner = n_dp - 1 - mate
    n_z, sides, depth, slabs, _ = sb.shape
    plane = sides // 2
    cap = depth // 2
    group = sides * cap
    rows = n_z * group
    tokens = x.shape[0]
    z, inner = lax.div(me, plane), lax.rem(me, plane)
    above, below = lax.rem(me + plane, n_exp), lax.rem(me + n_exp - plane, n_exp)
    quarter = wf.shape[1]
    half = quarter // 2
    ff = wf.shape[2] // 3
    per = slabs // n_dp
    others = n_exp - 1

    barrier = pltpu.get_barrier_semaphore()

    def greet(d, e):
        pl.semaphore_signal(
            barrier, inc=1, device_id={"dp": d, "expert": e}, device_id_type=MESH
        )

    def greet_both(i, carry):
        greet(my, lax.rem(me + i, n_exp))
        greet(partner, lax.rem(me + i, n_exp))
        return carry

    greet(mate, me)
    greet(corner, me)
    greet(partner, me)
    lax.fori_loop(1, n_exp, greet_both, 0)
    for which, ref in enumerate((x, g)):
        for a in range(slabs):
            sums[pl.ds(a, tokens, stride=slabs), :] = ref[:, a * LANES : (a + 1) * LANES].astype(F32)
        block[which * tokens : (which + 1) * tokens] = (
            sums[...].astype(BF16).reshape(tokens, slabs, LANES)
        )
    block[2 * tokens] = jnp.zeros((slabs, LANES), BF16)
    pl.semaphore_wait(barrier, 2 * n_exp + 1)

    def to(src, dst, ss, rs, d, e):
        return pltpu.make_async_remote_copy(
            src, dst, ss, rs, device_id={"dp": d, "expert": e}, device_id_type=MESH
        )

    def wait_for(ref, sem):
        pltpu.make_async_copy(ref, ref, sem).wait()

    parts = (pl.ds(0, tokens), pl.ds(tokens, tokens))
    steps = n_z // 2
    up = [block] + list(blocks[: steps - 1])
    down = [block] + list(blocks[steps - 1 : 2 * steps - 2])
    opposite = blocks[2 * steps - 2]

    def hop(t, n, part):
        if t == steps - 1:
            return opposite.at[parts[part]] if part == n else None
        return (up, down)[n][t + 1].at[parts[part]]

    def ring(t, n, part):
        target = hop(t, n, part)
        if target is not None:
            source = (up, down)[n][t].at[parts[part]]
            to(
                source, target, ring_ss.at[n, t, part], ring_rs.at[n, t, part], my, (above, below)[n]
            ).start()

    def ring_wait(t, n, part):
        target = hop(t, n, part)
        if target is not None:
            wait_for(target, ring_rs.at[n, t, part])

    ways = [(n, part) for part in range(2) for n in range(2)]

    def share(rel, held):
        def one(d, carry):
            for side, s in enumerate((slot, other_slot)):
                first = (2 * d + s) * cap
                for c in range(cap):
                    token = jnp.clip(table_smem[rel, 0, first + c], 0, 2 * tokens)
                    sb[rel, side * plane + d, c] = held[token]
                    sb[rel, side * plane + d, cap + c] = held[
                        jnp.minimum(token + tokens, 2 * tokens)
                    ]
            return carry

        lax.fori_loop(0, plane, one, 0)

        def out(i, carry):
            d = lax.rem(inner + i, plane)
            for side, y in enumerate((my, partner)):
                to(
                    sb.at[rel, side * plane + d],
                    recv.at[rel, side * plane + inner],
                    tok_ss,
                    tok_rs.at[rel],
                    y,
                    z * plane + d,
                ).start()
            return carry

        to(
            sb.at[rel, plane + inner],
            recv.at[rel, plane + inner],
            tok_ss,
            tok_rs.at[rel],
            partner,
            me,
        ).start()
        lax.fori_loop(1, plane, out, 0)
        recv[rel, inner] = sb[rel, inner]

    fanout = te.shape[0]
    last_dims = (((1,), (1,)), ((), ()))

    def route():
        ids = lambda count: lax.broadcasted_iota(jnp.int32, (count, tokens), 0)
        flag = lambda hit: hit.astype(F32).astype(BF16)
        matmul = lambda a, b: jnp.dot(a, b, preferred_element_type=F32)
        experts, replicas = proj.shape[0], copies.shape[1] // proj.shape[0]
        logits = lax.dot_general(proj[...], x[...], last_dims, preferred_element_type=F32)
        chosen = jnp.concatenate(
            [
                jnp.sum(
                    jnp.where(te[k : k + 1, :] == ids(experts), logits, 0.0), axis=0, keepdims=True
                )
                for k in range(fanout)
            ],
            axis=0,
        )
        powers = jnp.exp(chosen - jnp.max(chosen, axis=0, keepdims=True))
        probs[...] = powers / jnp.sum(powers, axis=0, keepdims=True)
        slot_row = jnp.broadcast_to(copies[...].astype(F32), (16, copies.shape[1])).astype(BF16)
        quota_row = jnp.broadcast_to(quotas[...].astype(F32), (16, quotas.shape[1])).astype(BF16)
        targets, hits = [], []
        for k in range(fanout):
            pick = te[k : k + 1, :] * replicas + choice[k : k + 1, :]
            target = matmul(slot_row, flag(pick == ids(copies.shape[1])))[0:1].astype(jnp.int32)
            targets.append(target)
            hits.append(target == ids(quotas.shape[1]))
        count = sum(hit.astype(F32) for hit in hits).astype(BF16)
        earlier = lax.broadcasted_iota(jnp.int32, (tokens, tokens), 0) < lax.broadcasted_iota(
            jnp.int32, (tokens, tokens), 1
        )
        ahead = matmul(count, flag(earlier))
        value = 2 * tokens - lax.broadcasted_iota(jnp.int32, (n_z, tokens), 1)
        picks = jnp.zeros((n_z, LANES), F32)
        weights = jnp.zeros((n_z, LANES), F32)
        n_slots = w.shape[0]
        for k in range(fanout):
            arrival = jnp.sum(jnp.where(hits[k], ahead, 0.0), axis=0, keepdims=True)
            kept = arrival < matmul(quota_row, flag(hits[k]))[0:1]
            arrival = arrival.astype(jnp.int32)
            owner, local = lax.div(targets[k], n_slots), lax.rem(targets[k], n_slots)
            to_plane = jnp.where(kept, lax.div(owner, plane), -1)
            spot_lane = (lax.rem(owner, plane) * n_slots + local) * cap + arrival
            plane_of[k : k + 1, :] = to_plane
            lane[k : k + 1, :] = spot_lane
            spots_of[k : k + 1, :] = jnp.where(
                kept, (local * n_exp + owner) * cap + arrival, n_slots * n_exp * cap
            )
            there = to_plane == ids(n_z)
            spread = flag(spot_lane == ids(LANES))
            picks = picks + lax.dot_general(
                jnp.where(there, value, 0).astype(F32).astype(BF16),
                spread,
                last_dims,
                preferred_element_type=F32,
            )
            weights = weights + lax.dot_general(
                jnp.where(there, probs[k : k + 1, :], 0.0).astype(BF16),
                spread,
                last_dims,
                preferred_element_type=F32,
            )
        picks = jnp.clip(picks, 0.0, 2.0 * tokens).astype(jnp.int32)
        table[...] = jnp.clip(2 * tokens - picks, 0, 2 * tokens).reshape(table.shape)
        q_table[...] = weights.reshape(q_table.shape)

    for n, part in ways:
        ring(0, n, part)
    to(w.at[slot], wf.at[my], w_ss.at[0], w_rs.at[0], mate, me).start()
    to(w.at[other_slot], wf.at[my], w_ss.at[1], w_rs.at[1], partner, me).start()
    own_w = pltpu.make_async_copy(w.at[slot], wf.at[my], own_sem.at[0])
    own_w.start()
    route()
    to_place = pltpu.make_async_copy(spots_of, place, own_sem.at[2])
    to_place.start()
    for source, target, ss, rs in (
        (table, table_recv, table_ss, table_rs),
        (q_table, q_mid, qt_ss, qt_rs),
    ):
        for rel in range(1, n_z):
            to(
                source.at[lax.rem(z + rel, n_z)],
                target.at[n_z - rel],
                ss,
                rs,
                my,
                lax.rem(me + rel * plane, n_exp),
            ).start()
        target[0] = source[z]
    for held in blocks:
        held[2 * tokens] = jnp.zeros((slabs, LANES), BF16)
    back[2 * n_exp * cap] = jnp.zeros((slabs, LANES), BF16)
    wait_for(table_recv.at[pl.ds(0, n_z - 1)], table_rs)
    to_smem = pltpu.make_async_copy(table_recv, table_smem, own_sem.at[1])
    to_smem.start()
    wait_for(q_mid.at[pl.ds(0, n_z - 1)], qt_rs)

    def q_out(i, carry):
        e = z * plane + lax.rem(inner + i, plane)
        for side, y in enumerate((my, partner)):
            to(q_mid, q_all.at[side * plane + inner], q_ss, q_rs, y, e).start()
        return carry

    to(q_mid, q_all.at[plane + inner], q_ss, q_rs, partner, me).start()
    lax.fori_loop(1, plane, q_out, 0)
    q_all[inner] = q_mid[...]
    to_smem.wait()

    lanes = lax.broadcasted_iota(jnp.int32, (sides, LANES), 1)

    def to_matrix(rel, which, out):
        part = recv[rel, :, which * cap : (which + 1) * cap]
        flat[...] = part.astype(F32).reshape(group * slabs, LANES)

        def gather(p, carry):
            for b in range(per):
                for c in range(cap):
                    value = flat[pl.ds(c * slabs + p * per + b, sides, stride=cap * slabs), :]
                    first = rel * group + c * sides
                    out[p, first : first + sides, b * LANES : (b + 1) * LANES] = value.astype(BF16)
            return carry

        lax.fori_loop(0, n_dp, gather, 0)

    def process(rel):
        wait_for(recv.at[rel, pl.ds(0, sides - 1)], tok_rs.at[rel])
        here = slice(rel * group, (rel + 1) * group)
        to_matrix(rel, 0, xm)
        to_matrix(rel, 1, gm)
        weights = q_all[:, rel].reshape(sides, LANES)
        weight = jnp.concatenate(
            [
                jnp.sum(
                    jnp.where(lanes == (2 * inner + slot) * cap + c, weights, 0.0),
                    axis=1,
                    keepdims=True,
                )
                for c in range(cap)
            ],
            axis=0,
        )
        q_col[here] = jnp.broadcast_to(weight, (group, LANES))

        def project(p, carry):
            gate_up, down = carry
            gate_up = gate_up + jnp.dot(
                xm[p, here], wf[p, :, : 2 * ff], preferred_element_type=F32
            )
            down = down + jnp.dot(gm[p, here], wf[p, :, 2 * ff :], preferred_element_type=F32)
            return gate_up, down

        gate_up, down = lax.fori_loop(
            0, n_dp, project, (jnp.zeros((group, 2 * ff), F32), jnp.zeros((group, ff), F32))
        )
        gate, up_value = gate_up[:, :ff], gate_up[:, ff:]
        sig = jax.nn.sigmoid(gate)
        silu = gate * sig
        act = (silu * up_value).astype(BF16)
        act_s[here] = act
        grad = jnp.sum(act.astype(F32) * down, axis=1, keepdims=True).astype(BF16).astype(F32)
        act_grad = weight * down
        gu[here, :ff] = (act_grad * up_value * sig * (1.0 + gate * (1.0 - sig))).astype(BF16)
        gu[here, ff:] = (act_grad * silu).astype(BF16)
        grads = jnp.zeros((sides, LANES), F32)
        for c in range(cap):
            grads = jnp.where(
                lanes == (2 * inner + slot) * cap + c,
                grad[c * sides : (c + 1) * sides],
                grads,
            )
        pg[:, rel] = grads.reshape(sides, 1, LANES)

        def expand(p, carry):
            value = lax.dot_general(
                gu[here],
                wf[p, :, : 2 * ff],
                (((1,), (1,)), ((), ())),
                preferred_element_type=F32,
            )
            for b in range(per):
                for c in range(cap):
                    flat[pl.ds(c * slabs + p * per + b, sides, stride=cap * slabs), :] = value[
                        c * sides : (c + 1) * sides, b * LANES : (b + 1) * LANES
                    ]
            return carry

        lax.fori_loop(0, n_dp, expand, 0)
        dxs[rel] = flat[...].astype(BF16).reshape(sides, cap, slabs, LANES)

    def send_back(rel, source, target, ss, rs):
        first = lax.rem(z + rel, n_z) * plane

        def both(i, carry):
            d = lax.rem(inner + i, plane)
            for side, y in enumerate((my, partner)):
                to(source.at[rel, side * plane + d], target, ss, rs, y, first + d).start()
            return carry

        if rel:
            lax.fori_loop(0, plane, both, 0)
        else:
            to(source.at[rel, plane + inner], target, ss, rs, partner, me).start()
            lax.fori_loop(1, plane, both, 0)

    spot = slot * n_exp + me
    own_rows = pl.ds(spot * cap, cap)

    def dx_start(rel):
        send_back(rel, dxs, back.at[own_rows], dx_ss, dx_rs)
        if rel == 0:
            back[own_rows] = dxs[0, inner]

    def pg_first():
        def both(i, carry):
            d = lax.rem(inner + i, plane)
            for side, y in enumerate((my, partner)):
                to(
                    pg.at[side * plane + d],
                    pg_in.at[side * plane + inner],
                    pg_ss,
                    pg_rs,
                    y,
                    z * plane + d,
                ).start()
            return carry

        to(
            pg.at[plane + inner], pg_in.at[plane + inner], pg_ss, pg_rs, partner, me
        ).start()
        lax.fori_loop(1, plane, both, 0)
        pg_in[inner] = pg[inner]

    def pg_second():
        wait_for(pg_in.at[pl.ds(0, sides - 1)], pg_rs)
        pg_mid[...] = jnp.sum(pg_in[...], axis=0)
        for rel in range(1, n_z):
            to(
                pg_mid.at[rel],
                pg_recv.at[n_z - rel],
                pm_ss,
                pm_rs,
                my,
                lax.rem(me + rel * plane, n_exp),
            ).start()
        pg_recv[0] = pg_mid[0]

    def weight_grad(p):
        both = (((0,), (0,)), ((), ()))
        dwp[p, :, : 2 * ff] = lax.dot_general(
            xm[p], gu[...], both, preferred_element_type=F32
        ).astype(BF16)
        out_grad = jnp.concatenate(
            [
                (q_col[...] * gm[p, :, n * LANES : (n + 1) * LANES].astype(F32)).astype(BF16)
                for n in range(quarter // LANES)
            ],
            axis=1,
        )
        dwp[p, :, 2 * ff :] = lax.dot_general(
            out_grad, act_s[...], both, preferred_element_type=F32
        ).astype(BF16)

    share(0, block)
    waiting, done = [0], []
    for t in range(steps - 1):
        for n, part in ways:
            ring_wait(t, n, part)
            ring(t + 1, n, part)
        if t == 0:
            wait_for(wf.at[partner], w_rs.at[1])
            to(wf.at[partner], wf.at[partner], w_ss.at[2], w_rs.at[2], mate, me).start()
        share(n_z - t - 1, up[t + 1])
        share(t + 1, down[t + 1])
        if t == max(steps - 3, 0):
            own_w.wait()
            wait_for(wf.at[mate], w_rs.at[0])
            wait_for(wf.at[corner], w_rs.at[2])
            wait_for(q_all.at[pl.ds(0, sides - 1)], q_rs)
        if t >= steps - 3:
            for rel in waiting:
                process(rel)
            done += waiting
            waiting = []
        waiting += [n_z - t - 1, t + 1]
    for n, part in ways:
        ring_wait(steps - 1, n, part)
    share(steps, opposite)
    for rel in reversed(done[1:]):
        dx_start(rel)
    for rel in waiting:
        process(rel)
    process(steps)
    pg_first()

    def give(n, source, target, d):
        to(source, target, g_ss.at[n], g_rs.at[n], d, me).start()

    halves = [pl.ds(n * half, half) for n in range(2)]

    def relay(n):
        wait_for(from_mate.at[halves[n]], g_rs.at[n])
        dwp[partner, halves[n]] = (
            dwp[partner, halves[n]].astype(F32) + from_mate[halves[n]].astype(F32)
        ).astype(BF16)
        give(3 + n, dwp.at[partner, halves[n]], from_partner.at[halves[n]], partner)

    weight_grad(corner)
    for n in range(2):
        give(n, dwp.at[corner, halves[n]], from_mate.at[halves[n]], mate)
    for rel in waiting:
        dx_start(rel)
    dx_start(steps)
    weight_grad(mate)
    give(2, dwp.at[mate], from_mate2, mate)
    pg_second()
    weight_grad(partner)
    dx_start(0)
    relay(0)
    weight_grad(my)

    wait_for(pg_recv.at[pl.ds(0, n_z - 1)], pm_rs)
    grads = pg_recv[...].reshape(n_z, LANES).astype(BF16)
    first_dims = (((0,), (0,)), ((), ()))
    planes = lax.rem(lax.broadcasted_iota(jnp.int32, (n_z, tokens), 0) + z, n_z)
    spots = lax.broadcasted_iota(jnp.int32, (LANES, tokens), 0)
    experts = lax.broadcasted_iota(jnp.int32, (n_exp, tokens), 0)
    pair = []
    weighted = jnp.zeros((1, tokens), F32)
    for k in range(fanout):
        hit = (plane_of[k : k + 1, :] == planes).astype(F32).astype(BF16)
        spread = lax.dot_general(grads, hit, first_dims, preferred_element_type=F32)
        value = jnp.sum(
            jnp.where(lane[k : k + 1, :] == spots, spread, 0.0), axis=0, keepdims=True
        )
        pair.append(value)
        weighted = weighted + probs[k : k + 1, :] * value
    logit = jnp.zeros((n_exp, tokens), F32)
    for k in range(fanout):
        chosen = probs[k : k + 1, :] * (pair[k] - weighted)
        logit = logit + jnp.where(te[k : k + 1, :] == experts, chosen, 0.0)
    logit = logit.astype(BF16)
    for a in range(slabs):
        flat[pl.ds(a, n_exp, stride=slabs), :] = jnp.dot(
            logit, x[:, a * LANES : (a + 1) * LANES], preferred_element_type=F32
        )
    rt[...] = flat[pl.ds(0, n_exp * slabs), :].astype(BF16).reshape(rt.shape)

    def rt_out(i, carry):
        d = lax.rem(me + i, n_exp)
        to(rt.at[d], rt_recv.at[me], rt_ss, rt_rs, my, d).start()
        return carry

    lax.fori_loop(1, n_exp, rt_out, 0)
    rt_recv[me] = rt[me]
    relay(1)
    wait_for(rt_recv.at[pl.ds(0, others)], rt_rs)
    r2[0] = jnp.sum(rt_recv[...].astype(F32), axis=0)
    for n, d in enumerate((mate, partner, corner)):
        to(r2.at[0], r2.at[n + 1], r2_ss.at[n], r2_rs.at[n], d, me).start()

    wait_for(back.at[pl.ds(0, (2 * n_exp - 1) * cap)], dx_rs)

    to_place.wait()

    def combine(t, carry):
        def row(k):
            return back[jnp.clip(place[k, t], 0, 2 * n_exp * cap)].astype(F32)

        total = row(0)
        for k in range(1, fanout):
            total = total + row(k)
        sums[pl.ds(pl.multiple_of(t * slabs, slabs), slabs), :] = total
        return carry

    lax.fori_loop(0, tokens, combine, 0, unroll=4)
    for a in range(slabs):
        cols = slice(a * LANES, (a + 1) * LANES)
        routed = lax.dot_general(logit, proj[:, cols], first_dims, preferred_element_type=F32)
        token_grad[:, cols] = (sums[pl.ds(a, tokens, stride=slabs), :] + routed).astype(BF16)

    for n in range(n_dp - 1):
        wait_for(r2.at[n + 1], r2_rs.at[n])
    sums[pl.ds(0, slabs), :] = r2[0] + r2[1] + r2[2] + r2[3]
    share_rows = slabs // n_dp
    rcol[...] = sums[pl.ds(my * share_rows, share_rows), :]
    outs = (gate_grad, up_grad, down_grad)
    for n in range(2):
        wait_for(from_partner.at[halves[n]], g_rs.at[3 + n])
    for n, out in enumerate(outs):
        cols = slice(n * ff, (n + 1) * ff)
        out[other_slot] = from_partner[:, cols].astype(F32)
    wait_for(from_mate2, g_rs.at[2])
    for n, out in enumerate(outs):
        cols = slice(n * ff, (n + 1) * ff)
        out[slot] = dwp[my, :, cols].astype(F32) + from_mate2[:, cols].astype(F32)

    for t in range(steps):
        for n, part in ways:
            if hop(t, n, part) is not None:
                wait_for(block.at[parts[part]], ring_ss.at[n, t, part])
    wait_for(table.at[pl.ds(0, n_z - 1)], table_ss)
    wait_for(q_table.at[pl.ds(0, n_z - 1)], qt_ss)
    wait_for(q_all.at[pl.ds(0, sides - 1)], q_ss)
    for rel in range(n_z):
        wait_for(recv.at[rel, pl.ds(0, sides - 1)], tok_ss)
    for n in range(3):
        wait_for(wf.at[0], w_ss.at[n])
    for n in (0, 1, 3, 4):
        wait_for(from_mate.at[pl.ds(0, half)], g_ss.at[n])
    wait_for(from_mate2, g_ss.at[2])
    wait_for(back.at[pl.ds(0, (2 * n_exp - 1) * cap)], dx_ss)
    wait_for(pg_in.at[pl.ds(0, sides - 1)], pg_ss)
    wait_for(pg_mid.at[pl.ds(0, n_z - 1)], pm_ss)
    wait_for(rt.at[pl.ds(0, others)], rt_ss)
    for n in range(n_dp - 1):
        wait_for(r2.at[0], r2_ss.at[n])


def exchange(n_dp, n_exp, w, x, g, proj, te, choice, copies, quotas):
    slots, quarter, wide = w.shape
    cap = CAP
    slabs = x.shape[1] // LANES
    held = (2 * x.shape[0] + 1, slabs, LANES)
    n_z = n_exp // PLANE
    fanout = te.shape[0]
    sides = 2 * n_exp // n_z
    group = sides * cap
    rows = n_z * group
    ff = wide // 3
    tokens, width = x.shape
    vmem = pl.BlockSpec(memory_space=pltpu.VMEM)
    hbm = pl.BlockSpec(memory_space=pl.ANY)
    dma = pltpu.SemaphoreType.DMA
    return pl.pallas_call(
        functools.partial(exchange_kernel, n_dp, n_exp),
        out_shape=(
            jax.ShapeDtypeStruct((tokens, width), BF16),
            jax.ShapeDtypeStruct((slots, quarter, ff), F32),
            jax.ShapeDtypeStruct((slots, quarter, ff), F32),
            jax.ShapeDtypeStruct((slots, quarter, ff), F32),
            jax.ShapeDtypeStruct((slabs // n_dp, LANES), F32),
        ),
        in_specs=[hbm] + [vmem] * 7,
        out_specs=(vmem,) * 5,
        scratch_shapes=[
            pltpu.VMEM((n_z, 1, LANES), jnp.int32),
            pltpu.VMEM((n_z, 1, LANES), F32),
            pltpu.VMEM((fanout, tokens), jnp.int32),
            pltpu.VMEM((fanout, tokens), jnp.int32),
            pltpu.VMEM((fanout, tokens), F32),
            pltpu.VMEM((fanout, tokens), jnp.int32),
            pltpu.SMEM((fanout, tokens), jnp.int32),
            pltpu.VMEM(held, BF16),
            pltpu.VMEM((n_z, sides, 2 * cap, slabs, LANES), BF16),
            pltpu.VMEM((n_z, sides, 2 * cap, slabs, LANES), BF16),
            pltpu.VMEM((n_z, sides, cap, slabs, LANES), BF16),
            pltpu.VMEM((2 * n_exp * cap + 1, slabs, LANES), BF16),
            pltpu.VMEM((n_z, 1, LANES), jnp.int32),
            pltpu.SMEM((n_z, 1, LANES), jnp.int32),
            pltpu.VMEM((n_z, 1, LANES), F32),
            pltpu.VMEM((sides, n_z, 1, LANES), F32),
            pltpu.VMEM((n_dp, quarter, wide), BF16),
            pltpu.VMEM((max(group, n_exp) * slabs, LANES), F32),
            pltpu.VMEM((n_dp, rows, quarter), BF16),
            pltpu.VMEM((n_dp, rows, quarter), BF16),
            pltpu.VMEM((rows, 2 * ff), BF16),
            pltpu.VMEM((rows, ff), BF16),
            pltpu.VMEM((rows, LANES), F32),
            pltpu.VMEM((n_dp, quarter, wide), BF16),
            pltpu.VMEM((quarter, wide), BF16),
            pltpu.VMEM((quarter, wide), BF16),
            pltpu.VMEM((quarter, wide), BF16),
            pltpu.VMEM((sides, n_z, 1, LANES), F32),
            pltpu.VMEM((sides, n_z, 1, LANES), F32),
            pltpu.VMEM((n_z, 1, LANES), F32),
            pltpu.VMEM((n_z, 1, LANES), F32),
            pltpu.VMEM((n_exp, slabs, LANES), BF16),
            pltpu.VMEM((n_exp, slabs, LANES), BF16),
            pltpu.VMEM((n_dp, slabs, LANES), F32),
            pltpu.VMEM((tokens * slabs, LANES), F32),
            dma((2, n_z // 2, 2)),
            dma((2, n_z // 2, 2)),
            dma,
            dma,
            dma,
            dma,
            dma,
            dma,
            dma,
            dma((n_z,)),
            dma((3,)),
            dma((3,)),
            dma((5,)),
            dma((5,)),
            dma,
            dma,
            dma,
            dma,
            dma,
            dma,
            dma,
            dma,
            dma((n_dp - 1,)),
            dma((n_dp - 1,)),
            dma((3,)),
        ]
        + [pltpu.VMEM(held, BF16)] * (n_z - 1),
        compiler_params=pltpu.CompilerParams(
            collective_id=0, has_side_effects=True, vmem_limit_bytes=60 * 1024 * 1024
        ),
    )(w, x, g, proj, te, choice, copies, quotas)


def shards(
    n_dp,
    n_exp,
    layer_inputs,
    output_adjoint,
    dispatcher_projection,
    gating_kernel,
    expansion_kernel,
    contraction_kernel,
    token_experts,
    copy_choice_index,
    expert_copies,
    send_quotas,
):
    width = layer_inputs.shape[1]

    weights = jnp.concatenate(
        [gating_kernel, expansion_kernel, contraction_kernel], axis=2
    ).transpose(1, 0, 2)
    token_grad, gate_grad, up_grad, down_grad, router = exchange(
        n_dp,
        n_exp,
        weights,
        layer_inputs,
        output_adjoint,
        dispatcher_projection.T,
        token_experts.T,
        copy_choice_index.T,
        expert_copies.reshape(1, -1),
        send_quotas.reshape(1, -1),
    )
    gate_grad, up_grad, down_grad = (
        grad.transpose(1, 0, 2) for grad in (gate_grad, up_grad, down_grad)
    )
    router_grad = router.reshape(width // n_dp, 1)
    return (token_grad, gate_grad, up_grad, down_grad, router_grad)


def solution(mesh):
    return jax.shard_map(
        functools.partial(shards, mesh.shape["dp"], mesh.shape["expert"]),
        mesh=mesh,
        in_specs=(
            P(("dp", "expert"), None),
            P(("dp", "expert"), None),
            P(),
            P("dp", "expert", None),
            P("dp", "expert", None),
            P("dp", "expert", None),
            P(("dp", "expert"), None),
            P(("dp", "expert"), None),
            P(),
            P(),
        ),
        out_specs=(
            P(("dp", "expert"), None),
            P("dp", "expert", None),
            P("dp", "expert", None),
            P("dp", "expert", None),
            P("dp", "expert"),
        ),
        check_vma=False,
    )
```
